32 devices in a mesh: az: 4 (over z), rng: 2 (over x), dp: 4 (over y, core).
Axes of the slice: x: 2, y: 2, z: 4, core: 2. Of those that a mesh axis runs over, the one named last changes fastest.
Arguments:
- tokens: bfloat16 [4, 64, 32, 512], P('dp', 'az', 'rng'), may hold values from -6 to 6
- qkv_weight: bfloat16 [512, 1536], replicated, may hold values from -0.25 to 0.25
- out_weight: bfloat16 [512, 512], replicated, may hold values from -0.25 to 0.25
- relative_bias: float32 [8, 17, 17], replicated, may hold values from -4 to 260
- cotangent: bfloat16 [4, 64, 32, 512], P('dp', 'az', 'rng'), may hold values from -6 to 6
Outputs:
- grad_tokens: bfloat16 [4, 64, 32, 512], P('dp', 'az', 'rng')
- grad_qkv_weight: float32 [512, 1536], P(('az', 'rng'))
- grad_out_weight: float32 [512, 512], P(('az', 'rng'))
- grad_bias: float32 [8, 17, 17], replicated
The draws below stay inside these ranges and needn't reach their ends.
All inputs are finite; a program needn't handle non-finite values.
Results may differ from the reference program's by a relative error of at most 0.012.
Values may be sent and summed in bfloat16 or wider, within the bound.
A program may use at most 128 MiB of HBM per device.

```python
import math
import jax
import jax.numpy as jnp
from jax import lax

D = 512
HEADS = 8
SPAN = 17
NA = 64
NR = 32
BATCH = 4


def draw_relative_bias(key, part):
    shape_key = jax.random.fold_in(key, 0)
    cell_count = SPAN * SPAN
    flat_base = jnp.clip(jax.random.normal(shape_key, (HEADS, cell_count), jnp.float32), -4.0, 4.0)
    return flat_base.reshape(HEADS, SPAN, SPAN)


def level_of(key, shape, cuts, low, top_value):
    level, own = 1.0, jax.random.fold_in(key, 6)
    for axis_at, shards_of in cuts:
        heights = jnp.exp(jax.random.uniform(jax.random.fold_in(own, axis_at), (shards_of,), jnp.float32, low / len(cuts), top_value / len(cuts)))
        level = level * jnp.repeat(heights, shape[axis_at] // shards_of).reshape([-1 if axis == axis_at else 1 for axis in range(len(shape))])
    return level


def centred(rng, shape, spread, reach, cuts=(), kind=jnp.bfloat16):
    loudness = level_of(rng, shape, cuts, -0.22, 0.18) if cuts else 1.0
    drawn = jax.random.normal(rng, shape, jnp.float32) * spread * loudness
    return jnp.minimum(jnp.maximum(drawn, -reach), reach).astype(kind)


def setup_inputs(seed: int = 0) -> dict:
    key_list = jax.random.split(jax.random.key(seed), 6)
    return {
        "tokens": centred(key_list[0], (BATCH, NA, NR, D), 1.0, 6.0, ((0, 4), (1, 4), (2, 2))),
        "qkv_weight": centred(key_list[1], (D, 3 * D), D ** -0.5, 0.25),
        "out_weight": centred(key_list[2], (D, D), D ** -0.5, 0.25),
        "relative_bias": draw_relative_bias(jax.random.fold_in(key_list[5], 71), 0),
        "cotangent": centred(key_list[4], (BATCH, NA, NR, D), 1.0, 6.0, ((0, 4), (1, 4), (2, 2))),
    }


def starts(*values):
    return tuple((jnp.asarray(value).astype(jnp.int32) for value in values))

def selector(length, radius, present):
    span = 2 * radius + 1
    inner = jnp.arange(length)[:, None, None]
    outer = jnp.arange(length + 2 * radius)[None, :, None]
    offset = jnp.arange(span)[None, None, :]
    return ((outer - inner == offset) & present[None, :, None]).astype(jnp.float32)

def window(table, along, across):
    heads = table.shape[0]
    part_bias = jnp.einsum('hxy,jly->hxjl', table, across, precision=lax.Precision.HIGHEST)
    full_bias = jnp.einsum('ikx,hxjl->hijkl', along, part_bias, precision=lax.Precision.HIGHEST)
    row_total = along.shape[0] * across.shape[0]
    col_total = along.shape[1] * across.shape[1]
    inside = lax.optimization_barrier(jnp.sum(along, axis=2))[:, None, :, None] * lax.optimization_barrier(jnp.sum(across, axis=2))[None, :, None, :] > 0.5
    return (full_bias.reshape(heads, row_total, col_total), inside.reshape(row_total, col_total))

def bias_grad(d_score, along, across):
    heads = d_score.shape[0]
    shaped = d_score.reshape(heads, along.shape[0], across.shape[0], along.shape[1], across.shape[1])
    folded = jnp.einsum('hijkl,ikx->hxjl', shaped, along, precision=lax.Precision.HIGHEST)
    return jnp.einsum('hxjl,jly->hxy', folded, across, precision=lax.Precision.HIGHEST)

def query_side(queries, d_attended, key_rows, value_rows, bias, inside, scale):
    score = jnp.einsum('qhc,khc->hqk', queries.astype(jnp.float32), key_rows.astype(jnp.float32)) * scale + bias
    score = jnp.where(inside[None], score, -jnp.inf)
    top = lax.optimization_barrier(jnp.max(score, axis=2, keepdims=True))
    log_total = top + jnp.log(lax.optimization_barrier(jnp.sum(jnp.exp(score - top), axis=2, keepdims=True)))
    soft_prob = jnp.exp(score - log_total)
    prob_low = lax.optimization_barrier(soft_prob.astype(jnp.bfloat16))
    attended = jnp.einsum('hqk,khc->qhc', prob_low.astype(jnp.float32), value_rows.astype(jnp.float32)).astype(jnp.bfloat16)
    attended_wide = lax.optimization_barrier(attended).astype(jnp.float32)
    delta = jnp.einsum('qhc,qhc->hq', d_attended.astype(jnp.float32), attended_wide)
    d_prob = jnp.einsum('qhc,khc->hqk', d_attended.astype(jnp.float32), value_rows.astype(jnp.float32))
    d_score = soft_prob * (d_prob - delta[:, :, None])
    score_low = lax.optimization_barrier(d_score.astype(jnp.bfloat16))
    d_query = (jnp.einsum('hqk,khc->qhc', score_low.astype(jnp.float32), key_rows.astype(jnp.float32)) * scale).astype(jnp.bfloat16)
    return (attended, log_total[:, :, 0], delta, d_query, d_score)

def key_side(key_rows, value_rows, queries, d_attended, log_total, delta, bias, inside, scale):
    score = jnp.einsum('khc,qhc->hkq', key_rows.astype(jnp.float32), queries.astype(jnp.float32)) * scale + bias
    score = jnp.where(inside[None], score, -jnp.inf)
    soft_prob = jnp.exp(score - log_total[:, None, :])
    prob_low = lax.optimization_barrier(soft_prob.astype(jnp.bfloat16))
    d_prob = jnp.einsum('khc,qhc->hkq', value_rows.astype(jnp.float32), d_attended.astype(jnp.float32))
    d_score = soft_prob * (d_prob - delta[:, None, :])
    score_low = lax.optimization_barrier(d_score.astype(jnp.bfloat16))
    d_key = (jnp.einsum('hkq,qhc->khc', score_low.astype(jnp.float32), queries.astype(jnp.float32)) * scale).astype(jnp.bfloat16)
    d_value = jnp.einsum('hkq,qhc->khc', prob_low.astype(jnp.float32), d_attended.astype(jnp.float32)).astype(jnp.bfloat16)
    return (d_key, d_value)

def reference(tokens, qkv_weight, out_weight, relative_bias, cotangent):
    sweeps, azimuth, radial, width = tokens.shape
    heads = relative_bias.shape[0]
    radius = relative_bias.shape[1] // 2
    head_dim = width // heads
    scale = 1.0 / math.sqrt(head_dim)
    tile = 8
    count_all = sweeps * azimuth * radial
    flat_tokens = tokens.reshape(count_all, width)
    flat_cot = cotangent.reshape(count_all, width)
    projected = jnp.dot(flat_tokens, qkv_weight, preferred_element_type=jnp.float32).astype(jnp.bfloat16)
    projected = projected.reshape(sweeps, azimuth, radial, 3 * width)
    queries = projected[..., :width]
    key_value = projected[..., width:]
    d_attended = lax.dot_general(flat_cot, out_weight, (((1,), (1,)), ((), ())), preferred_element_type=jnp.float32)
    d_attended = d_attended.astype(jnp.bfloat16).reshape(sweeps, azimuth, radial, width)

    def extend(field):
        wrapped = jnp.concatenate([field[:, azimuth - radius:], field, field[:, :radius]], axis=1)
        return jnp.pad(wrapped, ((0, 0), (0, 0), (radius, radius), (0, 0)))
    key_ext = extend(key_value)
    tiles_az = azimuth // tile
    tiles_rg = radial // tile
    tile_count = sweeps * tiles_az * tiles_rg
    ext_side = tile + 2 * radius
    along = selector(tile, radius, jnp.ones((ext_side,), dtype=bool))

    def locate(counter):
        sweep_at = counter // (tiles_az * tiles_rg)
        leftover = counter % (tiles_az * tiles_rg)
        return (sweep_at, leftover // tiles_rg * tile, leftover % tiles_rg * tile)

    def across_of(col_at):
        column = col_at - radius + jnp.arange(ext_side)
        return selector(tile, radius, (column >= 0) & (column < radial))

    def query_tile(counter):
        sweep_at, row_at, col_at = locate(counter)
        place = starts(sweep_at, row_at, col_at, 0)
        query_block = lax.dynamic_slice(queries, place, (1, tile, tile, width)).reshape(tile * tile, heads, head_dim)
        cot_block = lax.dynamic_slice(d_attended, place, (1, tile, tile, width)).reshape(tile * tile, heads, head_dim)
        pair_block = lax.dynamic_slice(key_ext, place, (1, ext_side, ext_side, 2 * width)).reshape(ext_side * ext_side, 2, heads, head_dim)
        across = across_of(col_at)
        bias, inside = window(relative_bias, along, across)
        attended, log_total, delta, d_query, d_score = query_side(query_block, cot_block, pair_block[:, 0], pair_block[:, 1], bias, inside, scale)
        return (attended.reshape(tile * tile, width), log_total.T, delta.T, d_query.reshape(tile * tile, width), bias_grad(d_score, along, across))
    group = math.gcd(tile_count, 64)

    def run_tiles(func):
        lanes = jnp.arange(tile_count, dtype=jnp.int32).reshape(tile_count // group, group)
        results = lax.map(jax.vmap(func), lanes)
        return jax.tree.map(lambda leaf: leaf.reshape((tile_count,) + leaf.shape[2:]), results)

    def untile(leaf):
        last = leaf.shape[-1]
        shaped = leaf.reshape(sweeps, tiles_az, tiles_rg, tile, tile, last)
        return shaped.transpose(0, 1, 3, 2, 4, 5).reshape(sweeps, azimuth, radial, last)
    attended_all, log_all, delta_all, dquery_all, bias_terms = run_tiles(query_tile)
    attended_all = untile(attended_all)
    log_all = untile(log_all)
    delta_all = untile(delta_all)
    dquery_all = untile(dquery_all)
    grad_bias = lax.optimization_barrier(jnp.sum(bias_terms, axis=0))
    pair_ext = extend(jnp.concatenate([queries, d_attended], axis=3))
    stats_ext = extend(jnp.concatenate([log_all, delta_all], axis=3))
    flipped = relative_bias[:, ::-1, ::-1]

    def key_tile(counter):
        sweep_at, row_at, col_at = locate(counter)
        place = starts(sweep_at, row_at, col_at, 0)
        own = lax.dynamic_slice(key_value, place, (1, tile, tile, 2 * width)).reshape(tile * tile, 2, heads, head_dim)
        near = lax.dynamic_slice(pair_ext, place, (1, ext_side, ext_side, 2 * width)).reshape(ext_side * ext_side, 2, heads, head_dim)
        near_stats = lax.dynamic_slice(stats_ext, place, (1, ext_side, ext_side, 2 * heads)).reshape(ext_side * ext_side, 2 * heads)
        across = across_of(col_at)
        bias, inside = window(flipped, along, across)
        d_key, d_value = key_side(own[:, 0], own[:, 1], near[:, 0], near[:, 1], near_stats[:, :heads].T, near_stats[:, heads:].T, bias, inside, scale)
        return jnp.stack([d_key, d_value], axis=1).reshape(tile * tile, 2 * width)
    grad_pair = untile(run_tiles(key_tile))
    grad_qkv = jnp.concatenate([dquery_all, grad_pair], axis=3)
    grad_flat = grad_qkv.reshape(count_all, 3 * width)
    grad_tokens = lax.dot_general(grad_flat, qkv_weight, (((1,), (1,)), ((), ())), preferred_element_type=jnp.float32)
    grad_tokens = grad_tokens.astype(jnp.bfloat16).reshape(sweeps, azimuth, radial, width)
    grad_qkv_weight = lax.dot_general(flat_tokens, grad_flat, (((0,), (0,)), ((), ())), preferred_element_type=jnp.float32)
    grad_out_weight = lax.dot_general(attended_all.reshape(count_all, width), flat_cot, (((0,), (0,)), ((), ())), preferred_element_type=jnp.float32)
    return (grad_tokens, grad_qkv_weight, grad_out_weight, grad_bias)
```

```python
import functools
import math

import jax
import jax.numpy as jnp
from jax import lax
from jax.experimental import pallas as pl
from jax.experimental.pallas import tpu as pltpu
from jax.sharding import PartitionSpec as P

MESH = pl.DeviceIdType.MESH
F32, BF16 = jnp.float32, jnp.bfloat16
NT = (((1,), (1,)), ((), ()))
HIGH = lax.Precision.HIGHEST


def mm(a, b):
    return jnp.dot(a, b, preferred_element_type=F32)


def mm_nt(a, b):
    return lax.dot_general(a, b, NT, preferred_element_type=F32)


class Copies:
    def __init__(self, send, recv):
        self.send, self.recv, self.count, self.made = send, recv, 0, []

    def put(self, src, dst, device):
        copy = pltpu.make_async_remote_copy(
            src_ref=src,
            dst_ref=dst,
            send_sem=self.send.at[self.count],
            recv_sem=self.recv.at[self.count],
            device_id=device,
            device_id_type=MESH,
        )
        copy.start()
        self.count += 1
        self.made.append(copy)
        return copy

    def drain(self):
        for copy in self.made:
            copy.wait_send()


def greet(devices):
    barrier = pltpu.get_barrier_semaphore()
    for device in devices:
        pl.semaphore_signal(barrier, inc=1, device_id=device, device_id_type=MESH)
    pl.semaphore_wait(barrier, len(devices))


def around(rings, rng_at, side):
    return lax.rem(rng_at + (1 if side else rings - 1), rings)


def halo_kernel(rows, rings, sides, tok, xo, xs, edge, send, recv, local):
    az, ring, dp = lax.axis_index("az"), lax.axis_index("rng"), lax.axis_index("dp")
    up, down = lax.rem(az + rows - 1, rows), lax.rem(az + 1, rows)
    others = [around(rings, ring, side) for side in range(sides)]
    greet(
        [(up, ring, dp), (down, ring, dp)]
        + [(at, other, dp) for other in others for at in (up, az, down)]
    )
    copies = Copies(send, recv)
    copies.put(tok.at[pl.ds(0, 128)], xo.at[pl.ds(384, 128)], (up, ring, dp))
    copies.put(tok.at[pl.ds(128, 128)], xo.at[pl.ds(0, 128)], (down, ring, dp))
    cells = tok[...].astype(F32).reshape(16, 16, 512)
    low = cells[:, :8].reshape(128, 512)
    high = cells[:, 8:].reshape(128, 512)
    for side in range(sides):
        if sides == 1:
            part = jnp.where(ring == 0, high, low)
            land = 0
        else:
            part = high if side else low
            land = 1 - side
        edge[side] = part.astype(BF16)
        src, dst, other = edge.at[side], xs.at[land], others[side]
        copies.put(src.at[pl.ds(0, 64)], dst.at[pl.ds(192, 64)], (up, other, dp))
        copies.put(src.at[pl.ds(64, 64)], dst.at[pl.ds(0, 64)], (down, other, dp))
        copies.put(src, dst.at[pl.ds(64, 128)], (az, other, dp))
    own = pltpu.make_async_copy(tok, xo.at[pl.ds(128, 256)], local)
    own.start()
    own.wait()
    for copy in copies.made:
        copy.wait()


def attend_kernel(
    rings, sides, xo, xs, cot, wqkv, wo, rb,
    own_ref, oh_ref, sh_ref, dq_ref, att_ref, gb_ref,
    kv, qs, da, tab, tables, bias, db,
):
    ring = lax.axis_index("rng")
    width = 16 + 8 * sides
    lane = lax.broadcasted_iota(jnp.int32, (1, 128), 1)
    group = lane // 16
    inner = lane - group * 16

    tab[...] = jnp.zeros_like(tab)
    for h in range(8):
        tab[h * 24 : h * 24 + 17, 0:17] = rb[h]

    def column(c):
        if c < 16:
            place = jnp.int32(c)
        elif sides == 1:
            place = jnp.where(ring == 0, c, c - 24)
        else:
            place = jnp.int32(c - 24 if c < 24 else c - 8)
        level = ring * 16 + place
        offset = place - inner + 8
        present = (level >= 0) & (level < rings * 16)
        valid = (offset >= 0) & (offset <= 16) & present
        offset = jnp.where(valid, offset, -1)
        hot = lax.broadcasted_iota(jnp.int32, (128, 128), 0) == offset
        return hot.astype(F32), valid

    for c in range(width):
        hot, valid = column(c)
        filled = jnp.dot(tab[...], hot, precision=HIGH, preferred_element_type=F32)
        tables[pl.ds(c, 192, width), :] = jnp.where(valid, filled, -jnp.inf)

    def pieces(a):
        found = [(a * 16, 16, 0)]
        for s in range(sides):
            found.append((384 + 192 * s + a * 8, 8, 16 + 8 * s))
        return found

    def build(p, carry):
        for hh in range(2):
            base = (2 * p + hh) * 24
            for a in range(24):
                block = jnp.full((width, 128), -jnp.inf, F32)
                for q in range(8):
                    i = a - q
                    if 0 <= i <= 16:
                        at = pl.multiple_of((base + i) * width, 8)
                        block = jnp.where(group == q, tables[pl.ds(at, width), :], block)
                for start, size, first in pieces(a):
                    bias[p, start : start + size, hh * 128 : hh * 128 + 128] = block[
                        first : first + size
                    ]
        return carry

    lax.fori_loop(0, 4, build, 0)

    def project(r, carry):
        at = pl.multiple_of(r * 128, 128)
        kv[pl.ds(at, 128), :] = mm(xo[pl.ds(at, 128), :], wqkv[:, 512:]).astype(BF16)
        return carry

    lax.fori_loop(0, 4, project, 0)
    for s in range(sides):

        def project_side(r, carry):
            at = pl.multiple_of(r * 128, 128)
            kv[pl.ds(512 + 256 * s + at, 128), :] = mm(
                xs[s, pl.ds(at, 128), :], wqkv[:, 512:]
            ).astype(BF16)
            return carry

        lax.fori_loop(0, 2, project_side, 0)
    qs[...] = (mm(xo[128:384, :], wqkv[:, :512]).astype(BF16).astype(F32) * 0.125).astype(BF16)
    da[...] = mm_nt(cot[...], wo[...]).astype(BF16)

    first_half = lax.broadcasted_iota(jnp.int32, (128, 128), 1) < 64

    def diagonal(block):
        wide = block.astype(F32)
        return jnp.concatenate(
            [jnp.where(first_half, wide, 0.0), jnp.where(first_half, 0.0, wide)], axis=0
        ).astype(BF16)

    def fold(block):
        return jnp.concatenate([block[:64, :128], block[64:, 128:]], axis=0)

    def gather(t, cols):
        parts = [kv[t * 128 : t * 128 + 384, cols]]
        for s in range(sides):
            parts.append(kv[512 + 256 * s + 64 * t : 704 + 256 * s + 64 * t, cols])
        return jnp.concatenate(parts, axis=0)

    def pair(p, carry):
        lanes = pl.ds(pl.multiple_of(p * 128, 128), 128)
        v_lanes = pl.ds(pl.multiple_of(512 + p * 128, 128), 128)
        grads = []
        for t in range(2):
            rows = slice(t * 128, t * 128 + 128)
            keys, values = gather(t, lanes), gather(t, v_lanes)
            query, d_out = diagonal(qs[rows, lanes]), diagonal(da[rows, lanes])
            score = mm_nt(keys, query) + bias[p]
            e = jnp.exp(score - jnp.max(score, axis=0, keepdims=True))
            prob = e * (1.0 / jnp.sum(e, axis=0, keepdims=True))
            prob_low = prob.astype(BF16)
            attended = fold(mm(values.T, prob_low)).astype(BF16)
            att_ref[lanes, rows] = attended
            terms = da[rows, lanes].astype(F32).T * attended.astype(F32)
            delta = jnp.concatenate(
                [
                    jnp.sum(terms[:64], axis=0, keepdims=True),
                    jnp.sum(terms[64:], axis=0, keepdims=True),
                ],
                axis=1,
            )
            d_score = prob * (mm_nt(values, d_out) - delta)
            if t == 0:
                db[p] = d_score
            else:
                db[p] = db[p] + d_score
            low = d_score.astype(BF16)
            d_query = fold(mm(keys.T, low)) * 0.125
            dq_ref[rows, lanes] = d_query.T.astype(BF16)
            grads.append((mm(low, query), mm(prob_low, d_out)))
        for kind, cols in ((0, lanes), (1, v_lanes)):
            g0, g1 = grads[0][kind], grads[1][kind]
            own_ref[:, cols] = g0[128:384] + g1[:256]
            oh_ref[0, :, cols] = g0[:128].astype(BF16)
            oh_ref[1, :, cols] = g1[256:384].astype(BF16)
            for s in range(sides):
                b = 384 + 192 * s
                sh_ref[s, 0:64, cols] = g0[b : b + 64].astype(BF16)
                sh_ref[s, 64:192, cols] = (g0[b + 64 : b + 192] + g1[b : b + 128]).astype(BF16)
                sh_ref[s, 192:256, cols] = g1[b + 128 : b + 192].astype(BF16)
        return carry

    lax.fori_loop(0, 4, pair, 0)

    def unbuild(p, carry):
        for hh in range(2):
            base = (2 * p + hh) * 24
            for i in range(17):
                block = jnp.zeros((width, 128), F32)
                for q in range(8):
                    found = [
                        db[p, start : start + size, hh * 128 : hh * 128 + 128]
                        for start, size, _ in pieces(i + q)
                    ]
                    block = jnp.where(group == q, jnp.concatenate(found, axis=0), block)
                tables[pl.ds(pl.multiple_of((base + i) * width, 8), width), :] = block
        return carry

    lax.fori_loop(0, 4, unbuild, 0)
    total = jnp.zeros((192, 128), F32)
    for c in range(width):
        hot, _ = column(c)
        total = total + lax.dot_general(
            tables[pl.ds(c, 192, width), :], hot, NT, precision=HIGH, preferred_element_type=F32
        )
    for h in range(8):
        gb_ref[h] = total[h * 24 : h * 24 + 17, 0:17]


def reduce_kernel(
    rows, rings, sides, share,
    own, oh, sh, dq, att, tok, cot, wqkv,
    gtok, gq, go,
    r_o, r_s, part, r1, ka, kb, rxa, ryb, a2, b2, rya, rxb, z3, rz, gath, send, recv,
):
    az, ring, dp = lax.axis_index("az"), lax.axis_index("rng"), lax.axis_index("dp")
    up, down = lax.rem(az + rows - 1, rows), lax.rem(az + 1, rows)
    others = [around(rings, ring, side) for side in range(sides)]
    y, core = dp // 2, lax.rem(dp, 2)
    mate, over = y * 2 + 1 - core, (1 - y) * 2 + core
    rng_to = [lax.rem(ring + o, rings) for o in range(1, rings)]
    az_to = [lax.rem(az + o, rows) for o in range(1, rows)]
    dp_to = [lax.rem(dp + o, 4) for o in range(1, 4)]
    greet(
        [(az, other, dp) for other in rng_to]
        + [(at, ring, dp) for at in az_to]
        + [(az, ring, other) for other in dp_to]
        + [(at, other, dp) for other in others for at in (up, down)]
    )
    copies = Copies(send, recv)
    back = [
        copies.put(oh.at[0], r_o.at[1], (up, ring, dp)),
        copies.put(oh.at[1], r_o.at[0], (down, ring, dp)),
    ]
    for s in range(sides):
        land = 0 if sides == 1 else 1 - s
        src, dst, other = sh.at[s], r_s.at[land], others[s]
        back.append(copies.put(src.at[pl.ds(0, 64)], dst.at[pl.ds(192, 64)], (up, other, dp)))
        back.append(copies.put(src.at[pl.ds(192, 64)], dst.at[pl.ds(0, 64)], (down, other, dp)))
        back.append(
            copies.put(src.at[pl.ds(64, 128)], dst.at[pl.ds(64, 128)], (az, other, dp))
        )
    box = (rows, rings, share, 512)
    tok_t = tok[...].T

    def pair_up(f):
        return copies.put(part.at[f, 1 - core], r1.at[f], (az, ring, mate))

    def spread(f, first):
        first.wait_recv()
        kept = part[f, core].astype(F32) + r1[f].astype(F32)
        ka[f] = kept[..., :256].astype(BF16)
        kb[f, 0] = kept[..., 256:384].astype(BF16)
        kb[f, 1] = kept[..., 384:].astype(BF16)
        over_x = [
            copies.put(ka.at[f, :, to], rxa.at[f, o], (az, to, dp)) for o, to in enumerate(rng_to)
        ]
        return over_x, copies.put(kb.at[f, 1 - y], ryb.at[f], (az, ring, over))

    def cross(f, state):
        over_x, over_y = state
        for copy in over_x:
            copy.wait_recv()
        kept = ka[f, :, ring].astype(F32)
        for o in range(rings - 1):
            kept = kept + rxa[f, o].astype(F32)
        a2[f, 0] = kept[..., :128].astype(BF16)
        a2[f, 1] = kept[..., 128:].astype(BF16)
        next_y = copies.put(a2.at[f, 1 - y], rya.at[f], (az, ring, over))
        over_y.wait_recv()
        b2[f] = (kb[f, y].astype(F32) + ryb[f].astype(F32)).astype(BF16)
        next_x = [
            copies.put(b2.at[f, :, to], rxb.at[f, o], (az, to, dp)) for o, to in enumerate(rng_to)
        ]
        return next_x, next_y

    def along(f, state):
        over_x, over_y = state
        over_y.wait_recv()
        z3[f, :, 0] = (a2[f, y].astype(F32) + rya[f].astype(F32)).astype(BF16)
        for copy in over_x:
            copy.wait_recv()
        kept = b2[f, :, ring].astype(F32)
        for o in range(rings - 1):
            kept = kept + rxb[f, o].astype(F32)
        z3[f, :, 1] = kept.astype(BF16)
        return [
            copies.put(z3.at[f, to], rz.at[f, o], (to, ring, dp)) for o, to in enumerate(az_to)
        ]

    def collect(f, state):
        for copy in state:
            copy.wait_recv()
        kept = z3[f, az].astype(F32)
        for o in range(rows - 1):
            kept = kept + rz[f, o].astype(F32)
        gath[f, dp] = kept.astype(BF16)
        return [
            copies.put(gath.at[f, dp], gath.at[f, dp], (az, ring, to)) for to in dp_to
        ]

    def finish(f, state):
        for copy in state:
            copy.wait_recv()
        for d in range(4):
            for sub in range(2):
                value = gath[f, d, sub].astype(F32)
                at = sub * 256 + (d // 2) * 128
                if f == 0 and d % 2 == 1:
                    go[:, at : at + 128] = value
                else:
                    start = at + (0 if f == 0 else 512 + 512 * (d % 2))
                    gq[:, start : start + 128] = value

    part[0, 0] = mm(tok_t, dq[...]).reshape(box).astype(BF16)
    part[0, 1] = mm(att[...], cot[...]).reshape(box).astype(BF16)
    s0 = pair_up(0)
    s0 = spread(0, s0)
    for copy in back:
        copy.wait_recv()
    grad = own[...] + jnp.concatenate([r_o[0], r_o[1]], axis=0).astype(F32)
    mids = []
    zero = jnp.zeros((16, 8, 1024), F32)
    for s in range(sides):
        got = r_s[s].astype(F32)
        mid = got[64:192] + jnp.concatenate([got[0:64], got[192:256]], axis=0)
        mids.append(mid.reshape(16, 8, 1024))
    if sides == 1:
        low = jnp.where(ring == 0, zero, mids[0])
        high = jnp.where(ring == 0, mids[0], zero)
    else:
        low, high = mids
    grad = grad + jnp.concatenate([low, high], axis=1).reshape(256, 1024)
    grad = grad.astype(BF16)
    part[1, 0] = mm(tok_t, grad[:, :512]).reshape(box).astype(BF16)
    part[1, 1] = mm(tok_t, grad[:, 512:]).reshape(box).astype(BF16)
    s1 = pair_up(1)
    s0 = cross(0, s0)
    s1 = spread(1, s1)
    gtok[...] = (
        mm_nt(dq[...], wqkv[:, :512])
        + mm_nt(grad[:, :512], wqkv[:, 512:1024])
        + mm_nt(grad[:, 512:], wqkv[:, 1024:])
    ).astype(BF16)
    s0 = along(0, s0)
    s1 = cross(1, s1)
    s0 = collect(0, s0)
    s1 = along(1, s1)
    finish(0, s0)
    s1 = collect(1, s1)
    finish(1, s1)
    copies.drain()


def vmem(count):
    return [pl.BlockSpec(memory_space=pltpu.VMEM)] * count


def shards(rows, rings, tokens, qkv_weight, out_weight, relative_bias, cotangent):
    sides = 1 if rings == 2 else 2
    share = 512 // (rows * rings)
    tok, cot = tokens.reshape(256, 512), cotangent.reshape(256, 512)
    shape = jax.ShapeDtypeStruct
    sems = pltpu.SemaphoreType.DMA
    count = 2 + 3 * sides
    limit = 48 * 1024 * 1024
    xo, xs = pl.pallas_call(
        functools.partial(halo_kernel, rows, rings, sides),
        out_shape=(shape((512, 512), BF16), shape((sides, 256, 512), BF16)),
        in_specs=vmem(1),
        out_specs=tuple(vmem(2)),
        scratch_shapes=[
            pltpu.VMEM((sides, 128, 512), BF16), sems((count,)), sems((count,)), sems,
        ],
        compiler_params=pltpu.CompilerParams(collective_id=0, has_side_effects=True),
        name="halo",
    )(tok)
    keys = 384 + 192 * sides
    own, oh, sh, dq, att, bias_part = pl.pallas_call(
        functools.partial(attend_kernel, rings, sides),
        out_shape=(
            shape((256, 1024), F32),
            shape((2, 128, 1024), BF16),
            shape((sides, 256, 1024), BF16),
            shape((256, 512), BF16),
            shape((512, 256), BF16),
            shape((8, 17, 17), F32),
        ),
        in_specs=vmem(6),
        out_specs=tuple(vmem(6)),
        scratch_shapes=[
            pltpu.VMEM((512 + 256 * sides, 1024), BF16),
            pltpu.VMEM((256, 512), BF16),
            pltpu.VMEM((256, 512), BF16),
            pltpu.VMEM((192, 128), F32),
            pltpu.VMEM((192 * (16 + 8 * sides), 128), F32),
            pltpu.VMEM((4, keys, 256), F32),
            pltpu.VMEM((4, keys, 256), F32),
        ],
        compiler_params=pltpu.CompilerParams(vmem_limit_bytes=limit),
        name="attend",
    )(xo, xs, cot, qkv_weight, out_weight, relative_bias)
    total_bias = lax.psum(bias_part, ("az", "rng", "dp"))
    count = 2 + 3 * sides + 2 * (1 + 2 * rings + (rows - 1) + 3)

    def buf(*dims):
        return pltpu.VMEM((2,) + dims, BF16)

    gtok, gq, go = pl.pallas_call(
        functools.partial(reduce_kernel, rows, rings, sides, share),
        out_shape=(
            shape((256, 512), BF16), shape((share, 1536), F32), shape((share, 512), F32),
        ),
        in_specs=vmem(8),
        out_specs=tuple(vmem(3)),
        scratch_shapes=[
            buf(128, 1024),
            pltpu.VMEM((sides, 256, 1024), BF16),
            buf(2, rows, rings, share, 512),
            buf(rows, rings, share, 512),
            buf(rows, rings, share, 256),
            buf(2, rows, rings, share, 128),
            buf(rings - 1, rows, share, 256),
            buf(rows, rings, share, 128),
            buf(2, rows, share, 128),
            buf(rows, rings, share, 128),
            buf(rows, share, 128),
            buf(rings - 1, rows, share, 128),
            buf(rows, 2, share, 128),
            buf(rows - 1, 2, share, 128),
            buf(4, 2, share, 128),
            sems((count,)),
            sems((count,)),
        ],
        compiler_params=pltpu.CompilerParams(
            collective_id=1, has_side_effects=True, vmem_limit_bytes=limit
        ),
        name="reduce",
    )(own, oh, sh, dq, att, tok, cot, qkv_weight)
    return gtok.reshape(tokens.shape), gq, go, total_bias


def solution(mesh):
    placed = (P("dp", "az", "rng", None), P(), P(), P(), P("dp", "az", "rng", None))
    return jax.shard_map(
        functools.partial(shards, mesh.shape["az"], mesh.shape["rng"]),
        mesh=mesh,
        in_specs=placed,
        out_specs=(P("dp", "az", "rng", None), P(("az", "rng"), None), P(("az", "rng"), None), P()),
        check_vma=False,
    )
```

```python
import functools
import math

import jax
import jax.numpy as jnp
from jax import lax
from jax.experimental import pallas as pl
from jax.experimental.pallas import tpu as pltpu
from jax.sharding import PartitionSpec as P

MESH = pl.DeviceIdType.MESH
F32, BF16 = jnp.float32, jnp.bfloat16
NT = (((1,), (1,)), ((), ()))
HIGH = lax.Precision.HIGHEST


def mm(a, b):
    return jnp.dot(a, b, preferred_element_type=F32)


def mm_nt(a, b):
    return lax.dot_general(a, b, NT, preferred_element_type=F32)


class Copies:
    def __init__(self, send, recv):
        self.send, self.recv, self.count, self.made = send, recv, 0, []

    def put(self, src, dst, device):
        copy = pltpu.make_async_remote_copy(
            src_ref=src,
            dst_ref=dst,
            send_sem=self.send.at[self.count],
            recv_sem=self.recv.at[self.count],
            device_id=device,
            device_id_type=MESH,
        )
        copy.start()
        self.count += 1
        self.made.append(copy)
        return copy

    def drain(self):
        for copy in self.made:
            copy.wait_send()


def greet(devices):
    barrier = pltpu.get_barrier_semaphore()
    for device in devices:
        pl.semaphore_signal(barrier, inc=1, device_id=device, device_id_type=MESH)
    pl.semaphore_wait(barrier, len(devices))


def around(rings, rng_at, side):
    return lax.rem(rng_at + (1 if side else rings - 1), rings)


def fused_kernel(
    rows, rings, sides, share,
    tok, wqkv_h, wo_h, rb, cot_h,
    gtok, gq, go, gb_ref,
    xo, xs, edge, wqkv, wo, cot, x_t,
    kv, qs, da, tab, tables, bias, db, dq, att, own, ext, r_o, r_s,
    part, r1, ka, kb, rx, ry, two, ry2, rx2, zin, rz, gath,
    bias_mine, bias_core, bias_y, bias_x, bias_z,
    send, recv, local,
):
    az, ring, dp = lax.axis_index("az"), lax.axis_index("rng"), lax.axis_index("dp")
    up, down = lax.rem(az + rows - 1, rows), lax.rem(az + 1, rows)
    others = [around(rings, ring, side) for side in range(sides)]
    y, core = dp // 2, lax.rem(dp, 2)
    mate, over = y * 2 + 1 - core, (1 - y) * 2 + core
    rng_to = [lax.rem(ring + o, rings) for o in range(1, rings)]
    az_to = [lax.rem(az + o, rows) for o in range(1, rows)]
    dp_to = [lax.rem(dp + o, 4) for o in range(1, 4)]
    loads = [
        pltpu.make_async_copy(tok, xo.at[pl.ds(128, 256)], local.at[0]),
        pltpu.make_async_copy(wqkv_h, wqkv, local.at[1]),
        pltpu.make_async_copy(cot_h, cot, local.at[2]),
        pltpu.make_async_copy(wo_h, wo, local.at[3]),
    ]
    for load in loads:
        load.start()
    greet(
        [(az, other, dp) for other in rng_to]
        + [(at, ring, dp) for at in az_to]
        + [(az, ring, other) for other in dp_to]
        + [(at, other, dp) for other in others for at in (up, down)]
    )
    copies = Copies(send, recv)
    halo = [
        copies.put(tok.at[pl.ds(0, 128)], xo.at[pl.ds(384, 128)], (up, ring, dp)),
        copies.put(tok.at[pl.ds(128, 128)], xo.at[pl.ds(0, 128)], (down, ring, dp)),
    ]
    loads[0].wait()
    cells = xo[128:384, :].astype(F32).reshape(16, 16, 512)
    low_cells = cells[:, :8].reshape(128, 512)
    high_cells = cells[:, 8:].reshape(128, 512)
    for side in range(sides):
        if sides == 1:
            chosen = jnp.where(ring == 0, high_cells, low_cells)
            land = 0
        else:
            chosen = high_cells if side else low_cells
            land = 1 - side
        edge[side] = chosen.astype(BF16)
        src, dst, other = edge.at[side], xs.at[land], others[side]
        halo.append(copies.put(src.at[pl.ds(0, 64)], dst.at[pl.ds(192, 64)], (up, other, dp)))
        halo.append(copies.put(src.at[pl.ds(64, 64)], dst.at[pl.ds(0, 64)], (down, other, dp)))
        halo.append(copies.put(src, dst.at[pl.ds(64, 128)], (az, other, dp)))

    width = 16 + 8 * sides
    lane = lax.broadcasted_iota(jnp.int32, (1, 128), 1)
    group = lane // 16
    inner = lane - group * 16

    tab[...] = jnp.zeros_like(tab)
    for h in range(8):
        tab[h * 24 : h * 24 + 17, 0:17] = rb[h]

    def column(c):
        if c < 16:
            place = jnp.int32(c)
        elif sides == 1:
            place = jnp.where(ring == 0, c, c - 24)
        else:
            place = jnp.int32(c - 24 if c < 24 else c - 8)
        level = ring * 16 + place
        offset = place - inner + 8
        present = (level >= 0) & (level < rings * 16)
        valid = (offset >= 0) & (offset <= 16) & present
        offset = jnp.where(valid, offset, -1)
        hot = lax.broadcasted_iota(jnp.int32, (128, 128), 0) == offset
        return hot.astype(F32), valid

    for c in range(width):
        hot, valid = column(c)
        filled = jnp.dot(tab[...], hot, precision=HIGH, preferred_element_type=F32)
        tables[pl.ds(c, 192, width), :] = jnp.where(valid, filled, -jnp.inf)

    def pieces(a):
        found = [(a * 16, 16, 0)]
        for s in range(sides):
            found.append((384 + 192 * s + a * 8, 8, 16 + 8 * s))
        return found

    def build(p, carry):
        for hh in range(2):
            base = (2 * p + hh) * 24
            for a in range(24):
                block = jnp.full((width, 128), -jnp.inf, F32)
                for q in range(8):
                    i = a - q
                    if 0 <= i <= 16:
                        at = pl.multiple_of((base + i) * width, 8)
                        block = jnp.where(group == q, tables[pl.ds(at, width), :], block)
                for start, size, first in pieces(a):
                    bias[p, start : start + size, hh * 128 : hh * 128 + 128] = block[
                        first : first + size
                    ]
        return carry

    lax.fori_loop(0, 4, build, 0)
    for load in loads[1:]:
        load.wait()
    tokens = xo[128:384, :]
    qs[...] = (mm(tokens, wqkv[:, :512]).astype(BF16).astype(F32) * 0.125).astype(BF16)
    kv[128:384, :] = mm(tokens, wqkv[:, 512:]).astype(BF16)
    da[...] = mm_nt(cot[...], wo[...]).astype(BF16)
    x_t[:, 128:384] = tokens.T
    for copy in halo:
        copy.wait_recv()
    for at in (0, 384):
        cells_at = xo[at : at + 128, :]
        kv[at : at + 128, :] = mm(cells_at, wqkv[:, 512:]).astype(BF16)
        x_t[:, at : at + 128] = cells_at.T
    for s in range(sides):
        at = 512 + 256 * s
        kv[at : at + 256, :] = mm(xs[s], wqkv[:, 512:]).astype(BF16)
        x_t[:, at : at + 256] = xs[s].T

    first_half = lax.broadcasted_iota(jnp.int32, (128, 128), 1) < 64

    def diagonal(block):
        wide = block.astype(F32)
        return jnp.concatenate(
            [jnp.where(first_half, wide, 0.0), jnp.where(first_half, 0.0, wide)], axis=0
        ).astype(BF16)

    def fold(block):
        return jnp.concatenate([block[:64, :128], block[64:, 128:]], axis=0)

    def gather(t, cols):
        parts = [kv[t * 128 : t * 128 + 384, cols]]
        for s in range(sides):
            parts.append(kv[512 + 256 * s + 64 * t : 704 + 256 * s + 64 * t, cols])
        return jnp.concatenate(parts, axis=0)

    def pair(half, p):
        lanes = pl.ds(pl.multiple_of(p * 128, 128), 128)
        v_lanes = pl.ds(pl.multiple_of(512 + p * 128, 128), 128)
        inside = p - 2 * half
        k_ext = pl.ds(pl.multiple_of(inside * 128, 128), 128)
        v_ext = pl.ds(pl.multiple_of(256 + inside * 128, 128), 128)
        grads = []
        for t in range(2):
            cut = slice(t * 128, t * 128 + 128)
            keys, values = gather(t, lanes), gather(t, v_lanes)
            query, d_out = diagonal(qs[cut, lanes]), diagonal(da[cut, lanes])
            score = mm_nt(keys, query) + bias[p]
            e = jnp.exp(score - jnp.max(score, axis=0, keepdims=True))
            prob = e * (1.0 / jnp.sum(e, axis=0, keepdims=True))
            prob_low = prob.astype(BF16)
            attended = fold(mm(values.T, prob_low)).astype(BF16)
            att[lanes, cut] = attended
            terms = da[cut, lanes].astype(F32).T * attended.astype(F32)
            delta = jnp.concatenate(
                [
                    jnp.sum(terms[:64], axis=0, keepdims=True),
                    jnp.sum(terms[64:], axis=0, keepdims=True),
                ],
                axis=1,
            )
            d_score = prob * (mm_nt(values, d_out) - delta)
            if t == 0:
                db[p] = d_score
            else:
                db[p] = db[p] + d_score
            low = d_score.astype(BF16)
            d_query = fold(mm(keys.T, low)) * 0.125
            dq[cut, lanes] = d_query.T.astype(BF16)
            grads.append((mm(low, query), mm(prob_low, d_out)))
        for kind, cols, wide in ((0, k_ext, lanes), (1, v_ext, v_lanes)):
            g0, g1 = grads[0][kind], grads[1][kind]
            mid = g0[128:384] + g1[:256]
            own[:, wide] = mid
            ext[half, 0:128, cols] = g0[:128].astype(BF16)
            ext[half, 128:384, cols] = mid.astype(BF16)
            ext[half, 384:512, cols] = g1[256:384].astype(BF16)
            for s in range(sides):
                b, e0 = 384 + 192 * s, 512 + 256 * s
                ext[half, e0 : e0 + 64, cols] = g0[b : b + 64].astype(BF16)
                ext[half, e0 + 64 : e0 + 192, cols] = (
                    g0[b + 64 : b + 192] + g1[b : b + 128]
                ).astype(BF16)
                ext[half, e0 + 192 : e0 + 256, cols] = g1[b + 128 : b + 192].astype(BF16)

    def send_back(half):
        src = ext.at[half]
        made = [
            copies.put(src.at[pl.ds(0, 128)], r_o.at[half, 1], (up, ring, dp)),
            copies.put(src.at[pl.ds(384, 128)], r_o.at[half, 0], (down, ring, dp)),
        ]
        for s in range(sides):
            e0 = 512 + 256 * s
            dst, other = r_s.at[half, 0 if sides == 1 else 1 - s], others[s]
            made.append(
                copies.put(src.at[pl.ds(e0, 64)], dst.at[pl.ds(192, 64)], (up, other, dp))
            )
            made.append(
                copies.put(src.at[pl.ds(e0 + 192, 64)], dst.at[pl.ds(0, 64)], (down, other, dp))
            )
            made.append(
                copies.put(src.at[pl.ds(e0 + 64, 128)], dst.at[pl.ds(64, 128)], (az, other, dp))
            )
        return made

    x_first = (False, True, False, True)

    def pair_up(u, grad):
        for c in range(2):
            block = grad[:, c * 256 : c * 256 + 256]
            part[u, c] = block.reshape(rows, rings, share, 256).astype(BF16)
        return copies.put(part.at[u, 1 - core], r1.at[u], (az, ring, mate))

    def spread(u, state):
        state.wait_recv()
        kept = part[u, core].astype(F32) + r1[u].astype(F32)
        if x_first[u]:
            ka[u] = kept.astype(BF16)
            return [
                copies.put(ka.at[u, :, to], rx.at[u, o], (az, to, dp))
                for o, to in enumerate(rng_to)
            ]
        kb[u, 0] = kept[..., :128].astype(BF16)
        kb[u, 1] = kept[..., 128:].astype(BF16)
        return [copies.put(kb.at[u, 1 - y], ry.at[u], (az, ring, over))]

    def cross(u, state):
        for copy in state:
            copy.wait_recv()
        if x_first[u]:
            kept = ka[u, :, ring].astype(F32)
            for o in range(rings - 1):
                kept = kept + rx[u, o].astype(F32)
            two[u, 0] = kept[..., :128].astype(BF16)
            two[u, 1] = kept[..., 128:].astype(BF16)
            return [copies.put(two.at[u, 1 - y], ry2.at[u], (az, ring, over))]
        kb[u, y] = (kb[u, y].astype(F32) + ry[u].astype(F32)).astype(BF16)
        return [
            copies.put(kb.at[u, y, :, to], rx2.at[u, o], (az, to, dp))
            for o, to in enumerate(rng_to)
        ]

    def along(u, state):
        for copy in state:
            copy.wait_recv()
        if x_first[u]:
            kept = two[u, y].astype(F32) + ry2[u].astype(F32)
        else:
            kept = kb[u, y, :, ring].astype(F32)
            for o in range(rings - 1):
                kept = kept + rx2[u, o].astype(F32)
        zin[u] = kept.astype(BF16)
        return [
            copies.put(zin.at[u, to], rz.at[u, o], (to, ring, dp)) for o, to in enumerate(az_to)
        ]

    def collect(u, state):
        for copy in state:
            copy.wait_recv()
        kept = zin[u, az].astype(F32)
        for o in range(rows - 1):
            kept = kept + rz[u, o].astype(F32)
        gath[u, dp] = kept.astype(BF16)
        return [copies.put(gath.at[u, dp], gath.at[u, dp], (az, ring, to)) for to in dp_to]

    def finish(u, state):
        for copy in state:
            copy.wait_recv()
        for d in range(4):
            value = gath[u, d].astype(F32)
            at_y, at_c = (d // 2) * 128, d % 2
            if u == 3:
                go[:, at_c * 256 + at_y : at_c * 256 + at_y + 128] = value
            else:
                start = at_c * 256 if u == 2 else 512 + 512 * at_c + 256 * u
                gq[:, start + at_y : start + at_y + 128] = value

    def looped(half):
        def step(p, carry):
            pair(half, p)
            return carry

        lax.fori_loop(2 * half, 2 * half + 2, step, 0)

    looped(0)
    back = send_back(0)
    u0 = pair_up(0, mm(x_t[...], ext[0]))
    looped(1)
    back += send_back(1)
    u0 = spread(0, u0)
    u1 = pair_up(1, mm(x_t[...], ext[1]))
    u2 = pair_up(2, mm(x_t[:, 128:384], dq[...]))
    u3 = pair_up(3, mm(att[...], cot[...]))
    u1 = spread(1, u1)
    u2 = spread(2, u2)
    u3 = spread(3, u3)

    def unbuild(p, carry):
        for hh in range(2):
            base = (2 * p + hh) * 24
            for i in range(17):
                block = jnp.zeros((width, 128), F32)
                for q in range(8):
                    found = [
                        db[p, start : start + size, hh * 128 : hh * 128 + 128]
                        for start, size, _ in pieces(i + q)
                    ]
                    block = jnp.where(group == q, jnp.concatenate(found, axis=0), block)
                tables[pl.ds(pl.multiple_of((base + i) * width, 8), width), :] = block
        return carry

    lax.fori_loop(0, 4, unbuild, 0)
    total = jnp.zeros((192, 128), F32)
    for c in range(width):
        hot, _ = column(c)
        total = total + lax.dot_general(
            tables[pl.ds(c, 192, width), :], hot, NT, precision=HIGH, preferred_element_type=F32
        )
    for h in range(8):
        bias_mine[0, :, h * 32 : h * 32 + 32] = total[h * 24 : h * 24 + 24, 0:32]
    b = copies.put(bias_mine.at[0], bias_core, (az, ring, mate))
    u0 = cross(0, u0)
    u1 = cross(1, u1)
    b.wait_recv()
    bias_mine[1] = bias_mine[0] + bias_core[...]
    b = copies.put(bias_mine.at[1], bias_y, (az, ring, over))
    u2 = cross(2, u2)
    u3 = cross(3, u3)
    b.wait_recv()
    bias_x[ring] = bias_mine[1] + bias_y[...]
    b = [copies.put(bias_x.at[ring], bias_x.at[ring], (az, to, dp)) for to in rng_to]
    u0 = along(0, u0)
    u1 = along(1, u1)
    for copy in b:
        copy.wait_recv()
    bias_z[az] = functools.reduce(jnp.add, [bias_x[r] for r in range(rings)])
    b = [copies.put(bias_z.at[az], bias_z.at[az], (to, ring, dp)) for to in az_to]
    u2 = along(2, u2)
    u3 = along(3, u3)
    u0 = collect(0, u0)
    u1 = collect(1, u1)

    for copy in back:
        copy.wait_recv()
    grads = []
    zero = jnp.zeros((16, 8, 512), F32)
    for half in range(2):
        grad = jnp.concatenate([r_o[half, 0], r_o[half, 1]], axis=0).astype(F32)
        mids = []
        for s in range(sides):
            got = r_s[half, s].astype(F32)
            mid = got[64:192] + jnp.concatenate([got[0:64], got[192:256]], axis=0)
            mids.append(mid.reshape(16, 8, 512))
        if sides == 1:
            low = jnp.where(ring == 0, zero, mids[0])
            high = jnp.where(ring == 0, mids[0], zero)
        else:
            low, high = mids
        grads.append(grad + jnp.concatenate([low, high], axis=1).reshape(256, 512))
    d_key = own[:, :512] + jnp.concatenate([grads[0][:, :256], grads[1][:, :256]], axis=1)
    d_value = own[:, 512:] + jnp.concatenate([grads[0][:, 256:], grads[1][:, 256:]], axis=1)
    gtok[...] = (
        mm_nt(dq[...], wqkv[:, :512])
        + mm_nt(d_key.astype(BF16), wqkv[:, 512:1024])
        + mm_nt(d_value.astype(BF16), wqkv[:, 1024:])
    ).astype(BF16)
    u2 = collect(2, u2)
    u3 = collect(3, u3)
    for copy in b:
        copy.wait_recv()
    summed = functools.reduce(jnp.add, [bias_z[a] for a in range(rows)])
    for h in range(8):
        gb_ref[h] = summed[0:17, h * 32 : h * 32 + 17]
    finish(0, u0)
    finish(1, u1)
    finish(2, u2)
    finish(3, u3)
    copies.drain()


def shards(rows, rings, tokens, qkv_weight, out_weight, relative_bias, cotangent):
    sides = 1 if rings == 2 else 2
    share = 512 // (rows * rings)
    tok, cot = tokens.reshape(256, 512), cotangent.reshape(256, 512)
    shape = jax.ShapeDtypeStruct
    sems = pltpu.SemaphoreType.DMA
    count = 2 + 3 * sides + 2 * (2 + 3 * sides)
    count += 4 * (1 + rings + rows + 2) + 2 + (rings - 1) + (rows - 1)
    keys, cells = 384 + 192 * sides, 512 + 256 * sides

    def low(*dims):
        return pltpu.VMEM(dims, BF16)

    def full(*dims):
        return pltpu.VMEM(dims, F32)

    hbm = pl.BlockSpec(memory_space=pl.ANY)
    vmem = pl.BlockSpec(memory_space=pltpu.VMEM)
    gtok, gq, go, gb = pl.pallas_call(
        functools.partial(fused_kernel, rows, rings, sides, share),
        out_shape=(
            shape((256, 512), BF16),
            shape((share, 1536), F32),
            shape((share, 512), F32),
            shape((8, 17, 17), F32),
        ),
        in_specs=[hbm, hbm, hbm, vmem, hbm],
        out_specs=(vmem, vmem, vmem, vmem),
        scratch_shapes=[
            low(512, 512),
            low(sides, 256, 512),
            low(sides, 128, 512),
            low(512, 1536),
            low(512, 512),
            low(256, 512),
            low(512, cells),
            low(cells, 1024),
            low(256, 512),
            low(256, 512),
            full(192, 128),
            full(192 * (16 + 8 * sides), 128),
            full(4, keys, 256),
            full(4, keys, 256),
            low(256, 512),
            low(512, 256),
            full(256, 1024),
            low(2, cells, 512),
            low(2, 2, 128, 512),
            low(2, sides, 256, 512),
            low(4, 2, rows, rings, share, 256),
            low(4, rows, rings, share, 256),
            low(4, rows, rings, share, 256),
            low(4, 2, rows, rings, share, 128),
            low(4, rings - 1, rows, share, 256),
            low(4, rows, rings, share, 128),
            low(4, 2, rows, share, 128),
            low(4, rows, share, 128),
            low(4, rings - 1, rows, share, 128),
            low(4, rows, share, 128),
            low(4, rows - 1, share, 128),
            low(4, 4, share, 128),
            full(2, 24, 256),
            full(24, 256),
            full(24, 256),
            full(rings, 24, 256),
            full(rows, 24, 256),
            sems((count,)),
            sems((count,)),
            sems((4,)),
        ],
        compiler_params=pltpu.CompilerParams(
            collective_id=0, has_side_effects=True, vmem_limit_bytes=48 * 1024 * 1024
        ),
        name="fused",
    )(tok, qkv_weight, out_weight, relative_bias, cot)
    return gtok.reshape(tokens.shape), gq, go, gb


def solution(mesh):
    placed = (P("dp", "az", "rng", None), P(), P(), P(), P("dp", "az", "rng", None))
    return jax.shard_map(
        functools.partial(shards, mesh.shape["az"], mesh.shape["rng"]),
        mesh=mesh,
        in_specs=placed,
        out_specs=(P("dp", "az", "rng", None), P(("az", "rng"), None), P(("az", "rng"), None), P()),
        check_vma=False,
    )
```

```python
import functools
import math

import jax
import jax.numpy as jnp
from jax import lax
from jax.experimental import pallas as pl
from jax.experimental.pallas import tpu as pltpu
from jax.sharding import PartitionSpec as P

MESH = pl.DeviceIdType.MESH
F32, BF16 = jnp.float32, jnp.bfloat16
NT = (((1,), (1,)), ((), ()))
HIGH = lax.Precision.HIGHEST


def mm(a, b):
    return jnp.dot(a, b, preferred_element_type=F32)


def mm_nt(a, b):
    return lax.dot_general(a, b, NT, preferred_element_type=F32)


class Copies:
    def __init__(self, send, recv):
        self.send, self.recv, self.count, self.made = send, recv, 0, []

    def put(self, src, dst, device):
        copy = pltpu.make_async_remote_copy(
            src_ref=src,
            dst_ref=dst,
            send_sem=self.send.at[self.count],
            recv_sem=self.recv.at[self.count],
            device_id=device,
            device_id_type=MESH,
        )
        copy.start()
        self.count += 1
        self.made.append(copy)
        return copy

    def drain(self):
        for copy in self.made:
            copy.wait_send()


def greet(devices):
    barrier = pltpu.get_barrier_semaphore()
    for device in devices:
        pl.semaphore_signal(barrier, inc=1, device_id=device, device_id_type=MESH)
    pl.semaphore_wait(barrier, len(devices))


def around(rings, rng_at, side):
    return lax.rem(rng_at + (1 if side else rings - 1), rings)


def fused_kernel(
    rows, rings, sides, share,
    tok, wqkv_h, wo_h, rb_h, cot_h,
    gtok, gq, go, gb_ref,
    xo, xs, edge, wqkv, wo, cot, rb, x_t,
    kv, qs, da, tab, tables, bias, db, dq, att, own, ext, r_o, r_s,
    part, r1, ka, kb, rx, ry, two, ry2, rx2, zin, rz, gath,
    bias_mine, bias_core, bias_y, bias_x, bias_z,
    send, recv, local,
):
    az, ring, dp = lax.axis_index("az"), lax.axis_index("rng"), lax.axis_index("dp")
    up, down = lax.rem(az + rows - 1, rows), lax.rem(az + 1, rows)
    others = [around(rings, ring, side) for side in range(sides)]
    y, core = dp // 2, lax.rem(dp, 2)
    mate, over = y * 2 + 1 - core, (1 - y) * 2 + core
    rng_to = [lax.rem(ring + o, rings) for o in range(1, rings)]
    az_to = [lax.rem(az + o, rows) for o in range(1, rows)]
    dp_to = [lax.rem(dp + o, 4) for o in range(1, 4)]
    loads = [
        pltpu.make_async_copy(tok, xo.at[pl.ds(128, 256)], local.at[0]),
        pltpu.make_async_copy(wqkv_h, wqkv, local.at[1]),
        pltpu.make_async_copy(cot_h, cot, local.at[2]),
        pltpu.make_async_copy(wo_h, wo, local.at[3]),
        pltpu.make_async_copy(rb_h, rb, local.at[4]),
    ]
    for load in loads:
        load.start()
    greet(
        [(az, other, dp) for other in rng_to]
        + [(at, ring, dp) for at in az_to]
        + [(az, ring, other) for other in dp_to]
        + [(at, other, dp) for other in others for at in (up, down)]
    )
    copies = Copies(send, recv)
    halo = [
        copies.put(tok.at[pl.ds(0, 128)], xo.at[pl.ds(384, 128)], (up, ring, dp)),
        copies.put(tok.at[pl.ds(128, 128)], xo.at[pl.ds(0, 128)], (down, ring, dp)),
    ]
    loads[0].wait()
    cells = xo[128:384, :].astype(F32).reshape(16, 16, 512)
    low_cells = cells[:, :8].reshape(128, 512)
    high_cells = cells[:, 8:].reshape(128, 512)
    for side in range(sides):
        if sides == 1:
            chosen = jnp.where(ring == 0, high_cells, low_cells)
            land = 0
        else:
            chosen = high_cells if side else low_cells
            land = 1 - side
        edge[side] = chosen.astype(BF16)
        src, dst, other = edge.at[side], xs.at[land], others[side]
        halo.append(copies.put(src.at[pl.ds(0, 64)], dst.at[pl.ds(192, 64)], (up, other, dp)))
        halo.append(copies.put(src.at[pl.ds(64, 64)], dst.at[pl.ds(0, 64)], (down, other, dp)))
        halo.append(copies.put(src, dst.at[pl.ds(64, 128)], (az, other, dp)))

    width = 16 + 8 * sides
    lane = lax.broadcasted_iota(jnp.int32, (1, 128), 1)
    group = lane // 16
    inner = lane - group * 16

    loads[4].wait()
    tab[...] = jnp.zeros_like(tab)
    tab[:, 0:17] = rb[...].reshape(136, 17)

    def column(c):
        if c < 16:
            place = jnp.int32(c)
        elif sides == 1:
            place = jnp.where(ring == 0, c, c - 24)
        else:
            place = jnp.int32(c - 24 if c < 24 else c - 8)
        level = ring * 16 + place
        offset = place - inner + 8
        present = (level >= 0) & (level < rings * 16)
        valid = (offset >= 0) & (offset <= 16) & present
        offset = jnp.where(valid, offset, -1)
        hot = lax.broadcasted_iota(jnp.int32, (128, 128), 0) == offset
        return hot.astype(F32), valid

    for c in range(width):
        hot, valid = column(c)
        filled = jnp.dot(tab[...], hot, precision=HIGH, preferred_element_type=F32)
        tables[pl.ds(c, 136, width), :] = jnp.where(valid, filled, -jnp.inf)

    def pieces(a):
        found = [(a * 16, 16, 0)]
        for s in range(sides):
            found.append((384 + 192 * s + a * 8, 8, 16 + 8 * s))
        return found

    def build(p, carry):
        for hh in range(2):
            head = 2 * p + hh
            for a in range(24):
                block = jnp.full((width, 128), -jnp.inf, F32)
                for q in range(8):
                    i = a - q
                    if 0 <= i <= 16:
                        at = pl.multiple_of((i * 8 + head) * width, 8)
                        block = jnp.where(group == q, tables[pl.ds(at, width), :], block)
                for start, size, first in pieces(a):
                    bias[p, start : start + size, hh * 128 : hh * 128 + 128] = block[
                        first : first + size
                    ]
        return carry

    lax.fori_loop(0, 4, build, 0)
    for load in loads[1:4]:
        load.wait()
    tokens = xo[128:384, :]
    qs[...] = (mm(tokens, wqkv[:, :512]).astype(BF16).astype(F32) * 0.125).astype(BF16)
    kv[128:384, :] = mm(tokens, wqkv[:, 512:]).astype(BF16)
    da[...] = mm_nt(cot[...], wo[...]).astype(BF16)
    x_t[:, 128:384] = tokens.T
    for copy in halo:
        copy.wait_recv()
    for at in (0, 384):
        cells_at = xo[at : at + 128, :]
        kv[at : at + 128, :] = mm(cells_at, wqkv[:, 512:]).astype(BF16)
        x_t[:, at : at + 128] = cells_at.T
    for s in range(sides):
        at = 512 + 256 * s
        kv[at : at + 256, :] = mm(xs[s], wqkv[:, 512:]).astype(BF16)
        x_t[:, at : at + 256] = xs[s].T

    first_half = lax.broadcasted_iota(jnp.int32, (128, 128), 1) < 64

    def diagonal(block):
        wide = block.astype(F32)
        return jnp.concatenate(
            [jnp.where(first_half, wide, 0.0), jnp.where(first_half, 0.0, wide)], axis=0
        ).astype(BF16)

    def fold(block):
        return jnp.concatenate([block[:64, :128], block[64:, 128:]], axis=0)

    def gather(t, cols):
        parts = [kv[t * 128 : t * 128 + 384, cols]]
        for s in range(sides):
            parts.append(kv[512 + 256 * s + 64 * t : 704 + 256 * s + 64 * t, cols])
        return jnp.concatenate(parts, axis=0)

    def pair(half, p):
        lanes = pl.ds(pl.multiple_of(p * 128, 128), 128)
        v_lanes = pl.ds(pl.multiple_of(512 + p * 128, 128), 128)
        inside = p - 2 * half
        k_ext = pl.ds(pl.multiple_of(inside * 128, 128), 128)
        v_ext = pl.ds(pl.multiple_of(256 + inside * 128, 128), 128)
        cuts = [slice(t * 128, t * 128 + 128) for t in range(2)]
        keys = [gather(t, lanes) for t in range(2)]
        values = [gather(t, v_lanes) for t in range(2)]
        query = [diagonal(qs[cut, lanes]) for cut in cuts]
        d_out = [diagonal(da[cut, lanes]) for cut in cuts]
        score = [mm_nt(keys[t], query[t]) + bias[p] for t in range(2)]
        e = [jnp.exp(x - jnp.max(x, axis=0, keepdims=True)) for x in score]
        d_prob = [mm_nt(values[t], d_out[t]) for t in range(2)]
        prob = [x * (1.0 / jnp.sum(x, axis=0, keepdims=True)) for x in e]
        prob_low = [x.astype(BF16) for x in prob]
        attended = [fold(mm(values[t].T, prob_low[t])).astype(BF16) for t in range(2)]
        d_value = [mm(prob_low[t], d_out[t]) for t in range(2)]
        terms = [da[cuts[t], lanes].astype(F32).T * attended[t].astype(F32) for t in range(2)]
        delta = [
            jnp.concatenate(
                [
                    jnp.sum(x[:64], axis=0, keepdims=True),
                    jnp.sum(x[64:], axis=0, keepdims=True),
                ],
                axis=1,
            )
            for x in terms
        ]
        d_score = [prob[t] * (d_prob[t] - delta[t]) for t in range(2)]
        low = [x.astype(BF16) for x in d_score]
        d_query = [fold(mm(keys[t].T, low[t])) * 0.125 for t in range(2)]
        d_key = [mm(low[t], query[t]) for t in range(2)]
        db[p] = d_score[0] + d_score[1]
        for t in range(2):
            att[lanes, cuts[t]] = attended[t]
            dq[cuts[t], lanes] = d_query[t].T.astype(BF16)
        grads = [(d_key[t], d_value[t]) for t in range(2)]
        for kind, cols, wide in ((0, k_ext, lanes), (1, v_ext, v_lanes)):
            g0, g1 = grads[0][kind], grads[1][kind]
            mid = g0[128:384] + g1[:256]
            own[:, wide] = mid
            ext[half, 0:128, cols] = g0[:128].astype(BF16)
            ext[half, 128:384, cols] = mid.astype(BF16)
            ext[half, 384:512, cols] = g1[256:384].astype(BF16)
            for s in range(sides):
                b, e0 = 384 + 192 * s, 512 + 256 * s
                ext[half, e0 : e0 + 64, cols] = g0[b : b + 64].astype(BF16)
                ext[half, e0 + 64 : e0 + 192, cols] = (
                    g0[b + 64 : b + 192] + g1[b : b + 128]
                ).astype(BF16)
                ext[half, e0 + 192 : e0 + 256, cols] = g1[b + 128 : b + 192].astype(BF16)

    def send_back(half):
        src = ext.at[half]
        made = [
            copies.put(src.at[pl.ds(0, 128)], r_o.at[half, 1], (up, ring, dp)),
            copies.put(src.at[pl.ds(384, 128)], r_o.at[half, 0], (down, ring, dp)),
        ]
        for s in range(sides):
            e0 = 512 + 256 * s
            dst, other = r_s.at[half, 0 if sides == 1 else 1 - s], others[s]
            made.append(
                copies.put(src.at[pl.ds(e0, 64)], dst.at[pl.ds(192, 64)], (up, other, dp))
            )
            made.append(
                copies.put(src.at[pl.ds(e0 + 192, 64)], dst.at[pl.ds(0, 64)], (down, other, dp))
            )
            made.append(
                copies.put(src.at[pl.ds(e0 + 64, 128)], dst.at[pl.ds(64, 128)], (az, other, dp))
            )
        return made

    x_first = (False, False, False, True)

    def pair_up(u, grad):
        for c in range(2):
            block = grad[:, c * 256 : c * 256 + 256]
            part[u, c] = block.reshape(rows, rings, share, 256).astype(BF16)
        return copies.put(part.at[u, 1 - core], r1.at[u], (az, ring, mate))

    def spread(u, state):
        state.wait_recv()
        kept = part[u, core].astype(F32) + r1[u].astype(F32)
        if x_first[u]:
            ka[u] = kept.astype(BF16)
            return [
                copies.put(ka.at[u, :, to], rx.at[u, o], (az, to, dp))
                for o, to in enumerate(rng_to)
            ]
        kb[u, 0] = kept[..., :128].astype(BF16)
        kb[u, 1] = kept[..., 128:].astype(BF16)
        return [copies.put(kb.at[u, 1 - y], ry.at[u], (az, ring, over))]

    def cross(u, state):
        for copy in state:
            copy.wait_recv()
        if x_first[u]:
            kept = ka[u, :, ring].astype(F32)
            for o in range(rings - 1):
                kept = kept + rx[u, o].astype(F32)
            two[u, 0] = kept[..., :128].astype(BF16)
            two[u, 1] = kept[..., 128:].astype(BF16)
            return [copies.put(two.at[u, 1 - y], ry2.at[u], (az, ring, over))]
        kb[u, y] = (kb[u, y].astype(F32) + ry[u].astype(F32)).astype(BF16)
        return [
            copies.put(kb.at[u, y, :, to], rx2.at[u, o], (az, to, dp))
            for o, to in enumerate(rng_to)
        ]

    def along(u, state):
        for copy in state:
            copy.wait_recv()
        if x_first[u]:
            kept = two[u, y].astype(F32) + ry2[u].astype(F32)
        else:
            kept = kb[u, y, :, ring].astype(F32)
            for o in range(rings - 1):
                kept = kept + rx2[u, o].astype(F32)
        zin[u] = kept.astype(BF16)
        return [
            copies.put(zin.at[u, to], rz.at[u, o], (to, ring, dp)) for o, to in enumerate(az_to)
        ]

    def collect(u, state):
        for copy in state:
            copy.wait_recv()
        kept = zin[u, az].astype(F32)
        for o in range(rows - 1):
            kept = kept + rz[u, o].astype(F32)
        gath[u, dp] = kept.astype(BF16)
        return [copies.put(gath.at[u, dp], gath.at[u, dp], (az, ring, to)) for to in dp_to]

    def finish(u, state):
        for copy in state:
            copy.wait_recv()
        for d in range(4):
            value = gath[u, d].astype(F32)
            at_y, at_c = (d // 2) * 128, d % 2
            if u == 3:
                go[:, at_c * 256 + at_y : at_c * 256 + at_y + 128] = value
            else:
                start = at_c * 256 if u == 2 else 512 + 512 * at_c + 256 * u
                gq[:, start + at_y : start + at_y + 128] = value

    def looped(half):
        def step(p, carry):
            pair(half, p)
            return carry

        lax.fori_loop(2 * half, 2 * half + 2, step, 0)

    looped(0)
    back = send_back(0)
    u0 = pair_up(0, mm(x_t[...], ext[0]))
    looped(1)
    back += send_back(1)
    u0 = spread(0, u0)
    u1 = pair_up(1, mm(x_t[...], ext[1]))
    u2 = pair_up(2, mm(x_t[:, 128:384], dq[...]))
    u3 = pair_up(3, mm(att[...], cot[...]))
    u1 = spread(1, u1)
    u2 = spread(2, u2)
    u3 = spread(3, u3)

    def unbuild(p, carry):
        for hh in range(2):
            head = 2 * p + hh
            for i in range(17):
                block = jnp.zeros((width, 128), F32)
                for q in range(8):
                    found = [
                        db[p, start : start + size, hh * 128 : hh * 128 + 128]
                        for start, size, _ in pieces(i + q)
                    ]
                    block = jnp.where(group == q, jnp.concatenate(found, axis=0), block)
                tables[pl.ds(pl.multiple_of((i * 8 + head) * width, 8), width), :] = block
        return carry

    lax.fori_loop(0, 4, unbuild, 0)
    total = jnp.zeros((136, 128), F32)
    for c in range(width):
        hot, _ = column(c)
        total = total + lax.dot_general(
            tables[pl.ds(c, 136, width), :], hot, NT, precision=HIGH, preferred_element_type=F32
        )
    for q in range(4):
        end = min(136, q * 40 + 40)
        bias_mine[0, 0 : end - q * 40, q * 32 : q * 32 + 32] = total[q * 40 : end, 0:32]
    bias_mine[0, 16:40, 96:128] = jnp.zeros((24, 32), F32)
    b = copies.put(bias_mine.at[0], bias_core, (az, ring, mate))
    u0 = cross(0, u0)
    u1 = cross(1, u1)
    b.wait_recv()
    bias_mine[1] = bias_mine[0] + bias_core[...]
    b = copies.put(bias_mine.at[1], bias_y, (az, ring, over))
    u2 = cross(2, u2)
    u3 = cross(3, u3)
    b.wait_recv()
    bias_x[ring] = bias_mine[1] + bias_y[...]
    b = [copies.put(bias_x.at[ring], bias_x.at[ring], (az, to, dp)) for to in rng_to]
    u0 = along(0, u0)
    u1 = along(1, u1)
    for copy in b:
        copy.wait_recv()
    bias_z[az] = functools.reduce(jnp.add, [bias_x[r] for r in range(rings)])
    b = [copies.put(bias_z.at[az], bias_z.at[az], (to, ring, dp)) for to in az_to]
    u2 = along(2, u2)
    u3 = along(3, u3)
    u0 = collect(0, u0)
    u1 = collect(1, u1)

    for copy in back:
        copy.wait_recv()
    grads = []
    zero = jnp.zeros((16, 8, 512), F32)
    for half in range(2):
        grad = jnp.concatenate([r_o[half, 0], r_o[half, 1]], axis=0).astype(F32)
        mids = []
        for s in range(sides):
            got = r_s[half, s].astype(F32)
            mid = got[64:192] + jnp.concatenate([got[0:64], got[192:256]], axis=0)
            mids.append(mid.reshape(16, 8, 512))
        if sides == 1:
            low = jnp.where(ring == 0, zero, mids[0])
            high = jnp.where(ring == 0, mids[0], zero)
        else:
            low, high = mids
        grads.append(grad + jnp.concatenate([low, high], axis=1).reshape(256, 512))
    d_key = own[:, :512] + jnp.concatenate([grads[0][:, :256], grads[1][:, :256]], axis=1)
    d_value = own[:, 512:] + jnp.concatenate([grads[0][:, 256:], grads[1][:, 256:]], axis=1)
    gtok[...] = (
        mm_nt(dq[...], wqkv[:, :512])
        + mm_nt(d_key.astype(BF16), wqkv[:, 512:1024])
        + mm_nt(d_value.astype(BF16), wqkv[:, 1024:])
    ).astype(BF16)
    u2 = collect(2, u2)
    u3 = collect(3, u3)
    for copy in b:
        copy.wait_recv()
    summed = functools.reduce(jnp.add, [bias_z[a] for a in range(rows)])
    for q in range(4):
        count = min(17, q * 5 + 5) - q * 5
        piece = summed[0 : count * 8, q * 32 : q * 32 + 17]
        gb_ref[q * 5 : q * 5 + count] = piece.reshape(count, 8, 17)
    finish(0, u0)
    finish(1, u1)
    finish(2, u2)
    finish(3, u3)
    copies.drain()


def shards(rows, rings, tokens, qkv_weight, out_weight, relative_bias, cotangent):
    sides = 1 if rings == 2 else 2
    share = 512 // (rows * rings)
    tok, cot = tokens.reshape(256, 512), cotangent.reshape(256, 512)
    shape = jax.ShapeDtypeStruct
    sems = pltpu.SemaphoreType.DMA
    count = 2 + 3 * sides + 2 * (2 + 3 * sides)
    count += 4 * (1 + rings + rows + 2) + 2 + (rings - 1) + (rows - 1)
    keys, cells = 384 + 192 * sides, 512 + 256 * sides

    def low(*dims):
        return pltpu.VMEM(dims, BF16)

    def full(*dims):
        return pltpu.VMEM(dims, F32)

    hbm = pl.BlockSpec(memory_space=pltpu.HBM)
    vmem = pl.BlockSpec(memory_space=pltpu.VMEM)
    gtok, gq, go, gb = pl.pallas_call(
        functools.partial(fused_kernel, rows, rings, sides, share),
        out_shape=(
            shape((256, 512), BF16),
            shape((share, 1536), F32),
            shape((share, 512), F32),
            shape((17, 8, 17), F32),
        ),
        in_specs=[hbm] * 5,
        out_specs=(vmem, vmem, vmem, vmem),
        scratch_shapes=[
            low(512, 512),
            low(sides, 256, 512),
            low(sides, 128, 512),
            low(512, 1536),
            low(512, 512),
            low(256, 512),
            full(17, 8, 17),
            low(512, cells),
            low(cells, 1024),
            low(256, 512),
            low(256, 512),
            full(136, 128),
            full(136 * (16 + 8 * sides), 128),
            full(4, keys, 256),
            full(4, keys, 256),
            low(256, 512),
            low(512, 256),
            full(256, 1024),
            low(2, cells, 512),
            low(2, 2, 128, 512),
            low(2, sides, 256, 512),
            low(4, 2, rows, rings, share, 256),
            low(4, rows, rings, share, 256),
            low(4, rows, rings, share, 256),
            low(4, 2, rows, rings, share, 128),
            low(4, rings - 1, rows, share, 256),
            low(4, rows, rings, share, 128),
            low(4, 2, rows, share, 128),
            low(4, rows, share, 128),
            low(4, rings - 1, rows, share, 128),
            low(4, rows, share, 128),
            low(4, rows - 1, share, 128),
            low(4, 4, share, 128),
            full(2, 40, 128),
            full(40, 128),
            full(40, 128),
            full(rings, 40, 128),
            full(rows, 40, 128),
            sems((count,)),
            sems((count,)),
            sems((5,)),
        ],
        compiler_params=pltpu.CompilerParams(
            collective_id=0, has_side_effects=True, vmem_limit_bytes=62 * 1024 * 1024
        ),
        name="fused",
    )(tok, qkv_weight, out_weight, relative_bias.transpose(1, 0, 2), cot)
    return gtok.reshape(tokens.shape), gq, go, gb.transpose(1, 0, 2)


def solution(mesh):
    placed = (P("dp", "az", "rng", None), P(), P(), P(), P("dp", "az", "rng", None))
    return jax.shard_map(
        functools.partial(shards, mesh.shape["az"], mesh.shape["rng"]),
        mesh=mesh,
        in_specs=placed,
        out_specs=(P("dp", "az", "rng", None), P(("az", "rng"), None), P(("az", "rng"), None), P()),
        check_vma=False,
    )
```

```python
import functools
import math

import jax
import jax.numpy as jnp
from jax import lax
from jax.experimental import pallas as pl
from jax.experimental.pallas import tpu as pltpu
from jax.sharding import PartitionSpec as P

MESH = pl.DeviceIdType.MESH
F32, BF16 = jnp.float32, jnp.bfloat16
NT = (((1,), (1,)), ((), ()))
HIGH = lax.Precision.HIGHEST


def mm(a, b):
    return jnp.dot(a, b, preferred_element_type=F32)


def mm_nt(a, b):
    return lax.dot_general(a, b, NT, preferred_element_type=F32)


class Copies:
    def __init__(self, send, recv):
        self.send, self.recv, self.count, self.made = send, recv, 0, []

    def put(self, src, dst, device):
        copy = pltpu.make_async_remote_copy(
            src_ref=src,
            dst_ref=dst,
            send_sem=self.send.at[self.count],
            recv_sem=self.recv.at[self.count],
            device_id=device,
            device_id_type=MESH,
        )
        copy.start()
        self.count += 1
        self.made.append(copy)
        return copy

    def drain(self):
        for copy in self.made:
            copy.wait_send()


def greet(devices):
    barrier = pltpu.get_barrier_semaphore()
    for device in devices:
        pl.semaphore_signal(barrier, inc=1, device_id=device, device_id_type=MESH)
    pl.semaphore_wait(barrier, len(devices))


def around(rings, rng_at, side):
    return lax.rem(rng_at + (1 if side else rings - 1), rings)


def fused_kernel(
    rows, rings, sides, share,
    tok, wqkv_h, wo_h, rb_h, cot_h,
    gtok, gq, go, gb_ref,
    xo, xs, edge, co, cs, cot_edge, wqkv, wo, rb, x_t,
    kv, qs, da, tab, tables, bias, back_bias, db, dq, att, own, ext,
    stat, stat_edge, stat_az, stat_rng, stat_ext,
    part, r1, ka, kb, rx, ry, two, ry2, rx2, zin, rz, gath,
    bias_mine, bias_core, bias_y, bias_x, bias_z,
    send, recv, local,
):
    az, ring, dp = lax.axis_index("az"), lax.axis_index("rng"), lax.axis_index("dp")
    up, down = lax.rem(az + rows - 1, rows), lax.rem(az + 1, rows)
    others = [around(rings, ring, side) for side in range(sides)]
    y, core = dp // 2, lax.rem(dp, 2)
    mate, over = y * 2 + 1 - core, (1 - y) * 2 + core
    rng_to = [lax.rem(ring + o, rings) for o in range(1, rings)]
    az_to = [lax.rem(az + o, rows) for o in range(1, rows)]
    dp_to = [lax.rem(dp + o, 4) for o in range(1, 4)]
    loads = [
        pltpu.make_async_copy(tok, xo.at[pl.ds(128, 256)], local.at[0]),
        pltpu.make_async_copy(wqkv_h, wqkv, local.at[1]),
        pltpu.make_async_copy(cot_h, co.at[pl.ds(128, 256)], local.at[2]),
        pltpu.make_async_copy(wo_h, wo, local.at[3]),
        pltpu.make_async_copy(rb_h, rb, local.at[4]),
    ]
    for load in loads:
        load.start()
    greet(
        [(az, other, dp) for other in rng_to]
        + [(at, ring, dp) for at in az_to]
        + [(az, ring, other) for other in dp_to]
        + [(at, other, dp) for other in others for at in (up, down)]
    )
    copies = Copies(send, recv)

    def edges(cells, depth):
        cells = cells.reshape(16, 16, depth)
        low, high = cells[:, :8].reshape(128, depth), cells[:, 8:].reshape(128, depth)
        return [jnp.where(ring == 0, high, low)] if sides == 1 else [low, high]

    def exchange(src, mid, side, edge, ready):
        made = [
            copies.put(src.at[pl.ds(0, 128)], mid.at[pl.ds(384, 128)], (up, ring, dp)),
            copies.put(src.at[pl.ds(128, 128)], mid.at[pl.ds(0, 128)], (down, ring, dp)),
        ]
        if ready is not None:
            ready.wait()
        for s, chosen in enumerate(edges(mid[128:384, :].astype(F32), 512)):
            edge[s] = chosen.astype(BF16)
            near, far, other = edge.at[s], side.at[0 if sides == 1 else 1 - s], others[s]
            made.append(copies.put(near.at[pl.ds(0, 64)], far.at[pl.ds(192, 64)], (up, other, dp)))
            made.append(copies.put(near.at[pl.ds(64, 64)], far.at[pl.ds(0, 64)], (down, other, dp)))
            made.append(copies.put(near, far.at[pl.ds(64, 128)], (az, other, dp)))
        return made

    halo = exchange(tok, xo, xs, edge, loads[0])

    width = 16 + 8 * sides
    lane = lax.broadcasted_iota(jnp.int32, (1, 128), 1)
    group = lane // 16
    inner = lane - group * 16

    loads[4].wait()
    tab[...] = jnp.zeros_like(tab)
    tab[:, 0:17] = rb[...].reshape(136, 17)

    def column(c, flipped=False):
        if c < 16:
            place = jnp.int32(c)
        elif sides == 1:
            place = jnp.where(ring == 0, c, c - 24)
        else:
            place = jnp.int32(c - 24 if c < 24 else c - 8)
        level = ring * 16 + place
        offset = place - inner + 8
        present = (level >= 0) & (level < rings * 16)
        valid = (offset >= 0) & (offset <= 16) & present
        offset = jnp.where(valid, 16 - offset if flipped else offset, -1)
        hot = lax.broadcasted_iota(jnp.int32, (128, 128), 0) == offset
        return hot.astype(F32), valid

    def fill(flipped):
        for c in range(width):
            hot, valid = column(c, flipped)
            filled = jnp.dot(tab[...], hot, precision=HIGH, preferred_element_type=F32)
            tables[pl.ds(c, 136, width), :] = jnp.where(valid, filled, -jnp.inf)

    def pieces(a):
        found = [(a * 16, 16, 0)]
        for s in range(sides):
            found.append((384 + 192 * s + a * 8, 8, 16 + 8 * s))
        return found

    def band(a, head, flipped):
        block = jnp.full((width, 128), -jnp.inf, F32)
        for q in range(8):
            i = a - q
            if 0 <= i <= 16:
                row = 16 - i if flipped else i
                at = pl.multiple_of((row * 8 + head) * width, 8)
                block = jnp.where(group == q, tables[pl.ds(at, width), :], block)
        return block

    def build(p, carry):
        for hh in range(2):
            for a in range(24):
                block = band(a, 2 * p + hh, False)
                for start, size, first in pieces(a):
                    bias[p, start : start + size, hh * 128 : hh * 128 + 128] = block[
                        first : first + size
                    ]
        return carry

    def build_back(p, carry):
        for hh in range(2):
            cols = slice(hh * 128, hh * 128 + 128)
            for a in range(24):
                block = band(a, 2 * p + hh, True)
                if a < 8:
                    back_bias[p, a * 16 : a * 16 + 16, cols] = block[:16]
                elif a >= 16:
                    back_bias[p, (a - 8) * 16 : (a - 8) * 16 + 16, cols] = block[:16]
                for s in range(sides):
                    start = 256 + 192 * s + a * 8
                    back_bias[p, start : start + 8, cols] = block[16 + 8 * s : 24 + 8 * s]
        return carry

    fill(True)
    lax.fori_loop(0, 4, build_back, 0)
    fill(False)
    lax.fori_loop(0, 4, build, 0)
    for load in loads[1:4]:
        load.wait()
    tokens = xo[128:384, :]

    def project(cells, at, size):
        made = mm(cells, wqkv[...]).astype(BF16)
        qs[at : at + size, :] = (made[:, :512].astype(F32) * 0.125).astype(BF16)
        kv[at : at + size, :] = made[:, 512:]
        x_t[:, at : at + size] = cells.T

    project(tokens, 128, 256)
    da[128:384, :] = mm_nt(co[128:384, :], wo[...]).astype(BF16)
    stat[...] = jnp.zeros_like(stat)
    for copy in halo:
        copy.wait_recv()
    cot_halo = exchange(cot_h, co, cs, cot_edge, None)
    for at in (0, 384):
        project(xo[at : at + 128, :], at, 128)
    for s in range(sides):
        project(xs[s], 512 + 256 * s, 256)

    first_half = lax.broadcasted_iota(jnp.int32, (128, 128), 1) < 64

    def diagonal(block):
        wide = block.astype(F32)
        return jnp.concatenate(
            [jnp.where(first_half, wide, 0.0), jnp.where(first_half, 0.0, wide)], axis=0
        ).astype(BF16)

    def fold(block):
        return jnp.concatenate([block[:64, :128], block[64:, 128:]], axis=0)

    def gather(t, cols):
        parts = [kv[t * 128 : t * 128 + 384, cols]]
        for s in range(sides):
            parts.append(kv[512 + 256 * s + 64 * t : 704 + 256 * s + 64 * t, cols])
        return jnp.concatenate(parts, axis=0)

    def pair(half, p):
        lanes = pl.ds(pl.multiple_of(p * 128, 128), 128)
        v_lanes = pl.ds(pl.multiple_of(512 + p * 128, 128), 128)
        inside = p - 2 * half
        k_ext = pl.ds(pl.multiple_of(inside * 128, 128), 128)
        v_ext = pl.ds(pl.multiple_of(256 + inside * 128, 128), 128)
        cuts = [slice(t * 128, t * 128 + 128) for t in range(2)]
        ext_cuts = [slice(t * 128 + 128, t * 128 + 256) for t in range(2)]
        keys = [gather(t, lanes) for t in range(2)]
        values = [gather(t, v_lanes) for t in range(2)]
        query = [diagonal(qs[cut, lanes]) for cut in ext_cuts]
        d_out = [diagonal(da[cut, lanes]) for cut in ext_cuts]
        score = [mm_nt(keys[t], query[t]) + bias[p] for t in range(2)]
        top = [jnp.max(x, axis=0, keepdims=True) for x in score]
        e = [jnp.exp(score[t] - top[t]) for t in range(2)]
        sums = [jnp.sum(x, axis=0, keepdims=True) for x in e]
        d_prob = [mm_nt(values[t], d_out[t]) for t in range(2)]
        prob = [e[t] * (1.0 / sums[t]) for t in range(2)]
        prob_low = [x.astype(BF16) for x in prob]
        attended = [fold(mm(values[t].T, prob_low[t])).astype(BF16) for t in range(2)]
        d_value = [mm(prob_low[t], d_out[t]) for t in range(2)]
        terms = [da[ext_cuts[t], lanes].astype(F32).T * attended[t].astype(F32) for t in range(2)]
        delta = [
            jnp.concatenate(
                [
                    jnp.sum(x[:64], axis=0, keepdims=True),
                    jnp.sum(x[64:], axis=0, keepdims=True),
                ],
                axis=1,
            )
            for x in terms
        ]
        d_score = [prob[t] * (d_prob[t] - delta[t]) for t in range(2)]
        low = [x.astype(BF16) for x in d_score]
        d_query = [fold(mm(keys[t].T, low[t])) * 0.125 for t in range(2)]
        d_key = [mm(low[t], query[t]) for t in range(2)]
        db[p] = d_score[0] + d_score[1]
        for t in range(2):
            att[lanes, cuts[t]] = attended[t]
            lse = top[t] + jnp.log(sums[t])
            for hh in range(2):
                side = slice(hh * 128, hh * 128 + 128)
                stat[t, p, hh : hh + 1, :] = lse[:, side]
                stat[t, p, 2 + hh : 3 + hh, :] = delta[t][:, side]
            dq[cuts[t], lanes] = d_query[t].T.astype(BF16)
        grads = [(d_key[t], d_value[t]) for t in range(2)]
        for kind, cols, wide in ((0, k_ext, lanes), (1, v_ext, v_lanes)):
            g0, g1 = grads[0][kind], grads[1][kind]
            mid = g0[128:384] + g1[:256]
            own[:, wide] = mid
            ext[half, 0:128, cols] = g0[:128].astype(BF16)
            ext[half, 128:384, cols] = mid.astype(BF16)
            ext[half, 384:512, cols] = g1[256:384].astype(BF16)
            for s in range(sides):
                b, e0 = 384 + 192 * s, 512 + 256 * s
                ext[half, e0 : e0 + 64, cols] = g0[b : b + 64].astype(BF16)
                ext[half, e0 + 64 : e0 + 192, cols] = (
                    g0[b + 64 : b + 192] + g1[b : b + 128]
                ).astype(BF16)
                ext[half, e0 + 192 : e0 + 256, cols] = g1[b + 128 : b + 192].astype(BF16)

    def send_stats():
        made = [
            copies.put(stat.at[0], stat_az.at[1], (up, ring, dp)),
            copies.put(stat.at[1], stat_az.at[0], (down, ring, dp)),
        ]
        columns = jnp.concatenate([stat[t].reshape(32, 128).T for t in range(2)], axis=0)
        for s, chosen in enumerate(edges(columns, 32)):
            stat_edge[s] = chosen.T
            near, far, other = stat_edge.at[s], stat_rng.at[0 if sides == 1 else 1 - s], others[s]
            made.append(copies.put(near, far.at[2], (up, other, dp)))
            made.append(copies.put(near, far.at[0], (down, other, dp)))
            made.append(copies.put(near, far.at[1], (az, other, dp)))
        return made

    def take_stats(made):
        for copy in made:
            copy.wait_recv()
        for t in range(2):
            stat_ext[t * 128 : t * 128 + 128, 0:32] = stat_az[t].reshape(32, 128).T
        for s in range(sides):
            e0 = 256 + 256 * s
            stat_ext[e0 : e0 + 64, 0:32] = stat_rng[s, 0].T[64:128]
            stat_ext[e0 + 64 : e0 + 192, 0:32] = stat_rng[s, 1].T
            stat_ext[e0 + 192 : e0 + 256, 0:32] = stat_rng[s, 2].T[0:64]

    def take_cotangent():
        for copy in cot_halo:
            copy.wait_recv()
        for at in (0, 384):
            da[at : at + 128, :] = mm_nt(co[at : at + 128, :], wo[...]).astype(BF16)
        for s in range(sides):
            at = 512 + 256 * s
            da[at : at + 256, :] = mm_nt(cs[s], wo[...]).astype(BF16)

    def back_pair(p):
        lanes = slice(p * 128, p * 128 + 128)
        v_lanes = slice(512 + p * 128, 640 + p * 128)

        def cells(ref, t, end, cols):
            found = [ref[t * end : t * end + 128, cols]]
            for s in range(sides):
                at = end + 128 + 256 * s + 64 * t
                found.append(ref[at : at + 192, cols])
            return jnp.concatenate(found, axis=0)

        def bands(t):
            found = [back_bias[p, t * 128 : t * 128 + 128, :]]
            for s in range(sides):
                found.append(back_bias[p, 256 + 192 * s : 448 + 192 * s, :])
            return jnp.concatenate(found, axis=0)

        def both(stats, k):
            return jnp.concatenate(
                [jnp.broadcast_to(stats[:, k + h : k + h + 1], (stats.shape[0], 128)) for h in (0, 1)],
                axis=1,
            )

        tiles = range(2)
        query = [cells(qs, t, 384, lanes) for t in tiles]
        d_out = [cells(da, t, 384, lanes) for t in tiles]
        stats = [cells(stat_ext, t, 128, slice(0, 32)) for t in tiles]
        mine = [slice(t * 128 + 128, t * 128 + 256) for t in tiles]
        keys = [diagonal(kv[cut, lanes]) for cut in mine]
        values = [diagonal(kv[cut, v_lanes]) for cut in mine]
        score = [mm_nt(query[t], keys[t]) + bands(t) for t in tiles]
        d_prob = [mm_nt(d_out[t], values[t]) for t in tiles]
        prob = [jnp.exp(score[t] - both(stats[t], p * 8)) for t in tiles]
        low = [
            (prob[t] * (d_prob[t] - both(stats[t], p * 8 + 2))).astype(BF16) for t in tiles
        ]
        d_key = [fold(mm(query[t].T, low[t])) for t in tiles]
        d_value = [fold(mm(d_out[t].T, prob[t].astype(BF16))) for t in tiles]
        for t in tiles:
            rows_at = slice(t * 128, t * 128 + 128)
            own[rows_at, lanes] = own[rows_at, lanes] + d_key[t].T
            own[rows_at, v_lanes] = own[rows_at, v_lanes] + d_value[t].T

    x_first = (False, False, False, True)

    def pair_up(u, grad):
        for c in range(2):
            block = grad[:, c * 256 : c * 256 + 256]
            part[u, c] = block.reshape(rows, rings, share, 256).astype(BF16)
        return copies.put(part.at[u, 1 - core], r1.at[u], (az, ring, mate))

    def spread(u, state):
        state.wait_recv()
        kept = part[u, core].astype(F32) + r1[u].astype(F32)
        if x_first[u]:
            ka[u] = kept.astype(BF16)
            return [
                copies.put(ka.at[u, :, to], rx.at[u, o], (az, to, dp))
                for o, to in enumerate(rng_to)
            ]
        kb[u, 0] = kept[..., :128].astype(BF16)
        kb[u, 1] = kept[..., 128:].astype(BF16)
        return [copies.put(kb.at[u, 1 - y], ry.at[u], (az, ring, over))]

    def cross(u, state):
        for copy in state:
            copy.wait_recv()
        if x_first[u]:
            kept = ka[u, :, ring].astype(F32)
            for o in range(rings - 1):
                kept = kept + rx[u, o].astype(F32)
            two[u, 0] = kept[..., :128].astype(BF16)
            two[u, 1] = kept[..., 128:].astype(BF16)
            return [copies.put(two.at[u, 1 - y], ry2.at[u], (az, ring, over))]
        kb[u, y] = (kb[u, y].astype(F32) + ry[u].astype(F32)).astype(BF16)
        return [
            copies.put(kb.at[u, y, :, to], rx2.at[u, o], (az, to, dp))
            for o, to in enumerate(rng_to)
        ]

    def along(u, state):
        for copy in state:
            copy.wait_recv()
        if x_first[u]:
            kept = two[u, y].astype(F32) + ry2[u].astype(F32)
        else:
            kept = kb[u, y, :, ring].astype(F32)
            for o in range(rings - 1):
                kept = kept + rx2[u, o].astype(F32)
        zin[u] = kept.astype(BF16)
        return [
            copies.put(zin.at[u, to], rz.at[u, o], (to, ring, dp)) for o, to in enumerate(az_to)
        ]

    def collect(u, state):
        for copy in state:
            copy.wait_recv()
        kept = zin[u, az].astype(F32)
        for o in range(rows - 1):
            kept = kept + rz[u, o].astype(F32)
        gath[u, dp] = kept.astype(BF16)
        return [copies.put(gath.at[u, dp], gath.at[u, dp], (az, ring, to)) for to in dp_to]

    def finish(u, state):
        for copy in state:
            copy.wait_recv()
        for d in range(4):
            value = gath[u, d].astype(F32)
            at_y, at_c = (d // 2) * 128, d % 2
            if u == 3:
                go[:, at_c * 256 + at_y : at_c * 256 + at_y + 128] = value
            else:
                start = at_c * 256 if u == 2 else 512 + 512 * at_c + 256 * u
                gq[:, start + at_y : start + at_y + 128] = value

    def looped(half):
        def step(p, carry):
            pair(half, p)
            return carry

        lax.fori_loop(2 * half, 2 * half + 2, step, 0)

    looped(0)
    u0 = pair_up(0, mm(x_t[...], ext[0]))
    looped(1)
    stats_out = send_stats()
    u0 = spread(0, u0)
    u1 = pair_up(1, mm(x_t[...], ext[1]))
    u2 = pair_up(2, mm(x_t[:, 128:384], dq[...]))
    u3 = pair_up(3, mm(att[...], co[128:384, :]))
    u1 = spread(1, u1)
    u2 = spread(2, u2)
    u3 = spread(3, u3)

    def unbuild(p, carry):
        for hh in range(2):
            head = 2 * p + hh
            for i in range(17):
                block = jnp.zeros((width, 128), F32)
                for q in range(8):
                    found = [
                        db[p, start : start + size, hh * 128 : hh * 128 + 128]
                        for start, size, _ in pieces(i + q)
                    ]
                    block = jnp.where(group == q, jnp.concatenate(found, axis=0), block)
                tables[pl.ds(pl.multiple_of((i * 8 + head) * width, 8), width), :] = block
        return carry

    lax.fori_loop(0, 4, unbuild, 0)
    total = jnp.zeros((136, 128), F32)
    for c in range(width):
        hot, _ = column(c)
        total = total + lax.dot_general(
            tables[pl.ds(c, 136, width), :], hot, NT, precision=HIGH, preferred_element_type=F32
        )
    for q in range(4):
        end = min(136, q * 40 + 40)
        bias_mine[0, 0 : end - q * 40, q * 32 : q * 32 + 32] = total[q * 40 : end, 0:32]
    bias_mine[0, 16:40, 96:128] = jnp.zeros((24, 32), F32)
    b = copies.put(bias_mine.at[0], bias_core, (az, ring, mate))
    u0 = cross(0, u0)
    take_cotangent()
    take_stats(stats_out)
    back_pair(0)
    b.wait_recv()
    bias_mine[1] = bias_mine[0] + bias_core[...]
    b = copies.put(bias_mine.at[1], bias_y, (az, ring, over))
    u1 = cross(1, u1)
    u3 = cross(3, u3)
    u0 = along(0, u0)
    back_pair(1)
    b.wait_recv()
    bias_x[ring] = bias_mine[1] + bias_y[...]
    b = [copies.put(bias_x.at[ring], bias_x.at[ring], (az, to, dp)) for to in rng_to]
    u2 = cross(2, u2)
    u1 = along(1, u1)
    back_pair(2)
    for copy in b:
        copy.wait_recv()
    bias_z[az] = functools.reduce(jnp.add, [bias_x[r] for r in range(rings)])
    b = [copies.put(bias_z.at[az], bias_z.at[az], (to, ring, dp)) for to in az_to]
    u3 = along(3, u3)
    u2 = along(2, u2)
    u0 = collect(0, u0)
    u1 = collect(1, u1)
    back_pair(3)
    u3 = collect(3, u3)
    u2 = collect(2, u2)
    gtok[...] = (
        mm_nt(dq[...], wqkv[:, :512])
        + mm_nt(own[:, :512].astype(BF16), wqkv[:, 512:1024])
        + mm_nt(own[:, 512:].astype(BF16), wqkv[:, 1024:])
    ).astype(BF16)
    for copy in b:
        copy.wait_recv()
    summed = functools.reduce(jnp.add, [bias_z[a] for a in range(rows)])
    for q in range(4):
        count = min(17, q * 5 + 5) - q * 5
        piece = summed[0 : count * 8, q * 32 : q * 32 + 17]
        gb_ref[q * 5 : q * 5 + count] = piece.reshape(count, 8, 17)
    finish(0, u0)
    finish(1, u1)
    finish(2, u2)
    finish(3, u3)
    copies.drain()


def leave_kernel(*refs):
    sem = refs[8]
    moves = [pltpu.make_async_copy(refs[i], refs[4 + i], sem.at[i]) for i in range(4)]
    for move in moves:
        move.start()
    for move in moves:
        move.wait()


def shards(rows, rings, tokens, qkv_weight, out_weight, relative_bias, cotangent):
    sides = 1 if rings == 2 else 2
    share = 512 // (rows * rings)
    tok, cot = tokens.reshape(256, 512), cotangent.reshape(256, 512)
    shape = jax.ShapeDtypeStruct
    sems = pltpu.SemaphoreType.DMA
    count = 2 + 3 * sides + 2 * (2 + 3 * sides)
    count += 4 * (1 + rings + rows + 2) + 2 + (rings - 1) + (rows - 1)
    keys, cells = 384 + 192 * sides, 512 + 256 * sides

    def low(*dims):
        return pltpu.VMEM(dims, BF16)

    def full(*dims):
        return pltpu.VMEM(dims, F32)

    hbm = pl.BlockSpec(memory_space=pltpu.HBM)
    vmem = pl.BlockSpec(memory_space=pltpu.VMEM)
    made = pl.pallas_call(
        functools.partial(fused_kernel, rows, rings, sides, share),
        out_shape=(
            shape((256, 512), BF16),
            shape((share, 1536), F32),
            shape((share, 512), F32),
            shape((17, 8, 17), F32),
        ),
        in_specs=[hbm] * 5,
        out_specs=(vmem, vmem, vmem, vmem),
        scratch_shapes=[
            low(512, 512),
            low(sides, 256, 512),
            low(sides, 128, 512),
            low(512, 512),
            low(sides, 256, 512),
            low(sides, 128, 512),
            low(512, 1536),
            low(512, 512),
            full(17, 8, 17),
            low(512, cells),
            low(cells, 1024),
            low(cells, 512),
            low(cells, 512),
            full(136, 128),
            full(136 * (16 + 8 * sides), 128),
            full(4, keys, 256),
            full(4, keys - 128, 256),
            full(4, keys, 256),
            low(256, 512),
            low(512, 256),
            full(256, 1024),
            low(2, cells, 512),
            full(2, 4, 8, 128),
            full(sides, 32, 128),
            full(2, 4, 8, 128),
            full(sides, 3, 32, 128),
            full(256 + 256 * sides, 128),
            low(4, 2, rows, rings, share, 256),
            low(4, rows, rings, share, 256),
            low(4, rows, rings, share, 256),
            low(4, 2, rows, rings, share, 128),
            low(4, rings - 1, rows, share, 256),
            low(4, rows, rings, share, 128),
            low(4, 2, rows, share, 128),
            low(4, rows, share, 128),
            low(4, rings - 1, rows, share, 128),
            low(4, rows, share, 128),
            low(4, rows - 1, share, 128),
            low(4, 4, share, 128),
            full(2, 40, 128),
            full(40, 128),
            full(40, 128),
            full(rings, 40, 128),
            full(rows, 40, 128),
            sems((count,)),
            sems((count,)),
            sems((5,)),
        ],
        compiler_params=pltpu.CompilerParams(
            collective_id=0, has_side_effects=True, vmem_limit_bytes=62 * 1024 * 1024
        ),
        name="fused",
    )(tok, qkv_weight, out_weight, relative_bias.transpose(1, 0, 2), cot)
    gtok, gq, go, gb = pl.pallas_call(
        leave_kernel,
        out_shape=tuple(shape(x.shape, x.dtype) for x in made),
        in_specs=[hbm] * 4,
        out_specs=(hbm,) * 4,
        scratch_shapes=[sems((4,))],
        compiler_params=pltpu.CompilerParams(vmem_limit_bytes=62 * 1024 * 1024),
        name="leave",
    )(*made)
    return gtok.reshape(tokens.shape), gq, go, gb.transpose(1, 0, 2)


def solution(mesh):
    placed = (P("dp", "az", "rng", None), P(), P(), P(), P("dp", "az", "rng", None))
    return jax.shard_map(
        functools.partial(shards, mesh.shape["az"], mesh.shape["rng"]),
        mesh=mesh,
        in_specs=placed,
        out_specs=(P("dp", "az", "rng", None), P(("az", "rng"), None), P(("az", "rng"), None), P()),
        check_vma=False,
    )
```

```python
import functools
import math

import jax
import jax.numpy as jnp
from jax import lax
from jax.experimental import pallas as pl
from jax.experimental.pallas import tpu as pltpu
from jax.sharding import PartitionSpec as P

MESH = pl.DeviceIdType.MESH
F32, BF16 = jnp.float32, jnp.bfloat16
NT = (((1,), (1,)), ((), ()))


def mm(a, b):
    return jnp.dot(a, b, preferred_element_type=F32)


def mm_nt(a, b):
    return lax.dot_general(a, b, NT, preferred_element_type=F32)


class Copies:
    def __init__(self, send, recv):
        self.send, self.recv, self.count, self.made = send, recv, 0, []

    def put(self, src, dst, device):
        copy = pltpu.make_async_remote_copy(
            src_ref=src,
            dst_ref=dst,
            send_sem=self.send.at[self.count],
            recv_sem=self.recv.at[self.count],
            device_id=device,
            device_id_type=MESH,
        )
        copy.start()
        self.count += 1
        self.made.append(copy)
        return copy

    def drain(self):
        for copy in self.made:
            copy.wait_send()


def greet(devices):
    barrier = pltpu.get_barrier_semaphore()
    for device in devices:
        pl.semaphore_signal(barrier, inc=1, device_id=device, device_id_type=MESH)
    pl.semaphore_wait(barrier, len(devices))


def around(rings, rng_at, side):
    return lax.rem(rng_at + (1 if side else rings - 1), rings)


def fused_kernel(
    rows, rings, sides, share,
    tok, wqkv_h, wo_h, rb_h, cot_h,
    gtok, gq, go, gb_ref,
    xo, xs, edge, wqkv, wo, cot, rb, x_t,
    kv, qs, da, tab, tables, bias, db, dq, att, own, ext, r_o, r_s,
    part, r1, ka, kb, rx, ry, two, ry2, rx2, zin, rz, gath,
    bias_mine, bias_core, bias_y, bias_x, bias_z,
    send, recv, local,
):
    az, ring, dp = lax.axis_index("az"), lax.axis_index("rng"), lax.axis_index("dp")
    up, down = lax.rem(az + rows - 1, rows), lax.rem(az + 1, rows)
    others = [around(rings, ring, side) for side in range(sides)]
    y, core = dp // 2, lax.rem(dp, 2)
    mate, over = y * 2 + 1 - core, (1 - y) * 2 + core
    rng_to = [lax.rem(ring + o, rings) for o in range(1, rings)]
    az_to = [lax.rem(az + o, rows) for o in range(1, rows)]
    dp_to = [lax.rem(dp + o, 4) for o in range(1, 4)]
    loads = [
        pltpu.make_async_copy(tok, xo.at[pl.ds(128, 256)], local.at[0]),
        pltpu.make_async_copy(wqkv_h, wqkv, local.at[1]),
        pltpu.make_async_copy(cot_h, cot, local.at[2]),
        pltpu.make_async_copy(wo_h, wo, local.at[3]),
        pltpu.make_async_copy(rb_h, rb, local.at[4]),
    ]
    for load in loads:
        load.start()
    greet(
        [(az, other, dp) for other in rng_to]
        + [(at, ring, dp) for at in az_to]
        + [(az, ring, other) for other in dp_to]
        + [(at, other, dp) for other in others for at in (up, down)]
    )
    copies = Copies(send, recv)
    halo = [
        copies.put(tok.at[pl.ds(0, 128)], xo.at[pl.ds(384, 128)], (up, ring, dp)),
        copies.put(tok.at[pl.ds(128, 128)], xo.at[pl.ds(0, 128)], (down, ring, dp)),
    ]
    loads[0].wait()
    cells = xo[128:384, :].astype(F32).reshape(16, 16, 512)
    low_cells = cells[:, :8].reshape(128, 512)
    high_cells = cells[:, 8:].reshape(128, 512)
    for side in range(sides):
        if sides == 1:
            chosen = jnp.where(ring == 0, high_cells, low_cells)
            land = 0
        else:
            chosen = high_cells if side else low_cells
            land = 1 - side
        edge[side] = chosen.astype(BF16)
        src, dst, other = edge.at[side], xs.at[land], others[side]
        halo.append(copies.put(src.at[pl.ds(0, 64)], dst.at[pl.ds(192, 64)], (up, other, dp)))
        halo.append(copies.put(src.at[pl.ds(64, 64)], dst.at[pl.ds(0, 64)], (down, other, dp)))
        halo.append(copies.put(src, dst.at[pl.ds(64, 128)], (az, other, dp)))

    width = 16 + 8 * sides
    lane = lax.broadcasted_iota(jnp.int32, (1, 128), 1)
    group = lane // 16
    inner = lane - group * 16

    loads[4].wait()
    tab[...] = jnp.zeros_like(tab)
    tab[:, 0:17] = rb[...].reshape(136, 17)

    def column(c):
        if c < 16:
            place = jnp.int32(c)
        elif sides == 1:
            place = jnp.where(ring == 0, c, c - 24)
        else:
            place = jnp.int32(c - 24 if c < 24 else c - 8)
        level = ring * 16 + place
        offset = place - inner + 8
        present = (level >= 0) & (level < rings * 16)
        valid = (offset >= 0) & (offset <= 16) & present
        offset = jnp.where(valid, offset, -1)
        hot = lax.broadcasted_iota(jnp.int32, (128, 128), 0) == offset
        return hot.astype(BF16), valid

    def split(block, count):
        found = []
        for _ in range(count):
            found.append(block.astype(BF16))
            block = block - found[-1].astype(F32)
        return jnp.concatenate(found, axis=0)

    tab_parts = split(tab[...], 3)
    for c in range(width):
        hot, valid = column(c)
        filled = mm(tab_parts, hot)
        filled = filled[:136] + filled[136:272] + filled[272:]
        tables[pl.ds(c, 136, width), :] = jnp.where(valid, filled, -jnp.inf)

    def pieces(a):
        found = [(a * 16, 16, 0)]
        for s in range(sides):
            found.append((384 + 192 * s + a * 8, 8, 16 + 8 * s))
        return found

    def build(p, carry):
        for hh in range(2):
            head = 2 * p + hh
            for a in range(24):
                block = jnp.full((width, 128), -jnp.inf, F32)
                for q in range(8):
                    i = a - q
                    if 0 <= i <= 16:
                        at = pl.multiple_of((i * 8 + head) * width, 8)
                        block = jnp.where(group == q, tables[pl.ds(at, width), :], block)
                for start, size, first in pieces(a):
                    bias[p, start : start + size, hh * 128 : hh * 128 + 128] = block[
                        first : first + size
                    ]
        return carry

    lax.fori_loop(0, 4, build, 0)
    for load in loads[1:4]:
        load.wait()
    tokens = xo[128:384, :]
    qs[...] = (mm(tokens, wqkv[:, :512]).astype(BF16).astype(F32) * 0.125).astype(BF16)
    kv[128:384, :] = mm(tokens, wqkv[:, 512:]).astype(BF16)
    da[...] = mm_nt(cot[...], wo[...]).astype(BF16)
    x_t[:, 128:384] = tokens.T
    for copy in halo:
        copy.wait_recv()
    for at in (0, 384):
        cells_at = xo[at : at + 128, :]
        kv[at : at + 128, :] = mm(cells_at, wqkv[:, 512:]).astype(BF16)
        x_t[:, at : at + 128] = cells_at.T
    for s in range(sides):
        at = 512 + 256 * s
        kv[at : at + 256, :] = mm(xs[s], wqkv[:, 512:]).astype(BF16)
        x_t[:, at : at + 256] = xs[s].T

    first_half = lax.broadcasted_iota(jnp.int32, (128, 128), 1) < 64

    def diagonal(block):
        wide = block.astype(F32)
        return jnp.concatenate(
            [jnp.where(first_half, wide, 0.0), jnp.where(first_half, 0.0, wide)], axis=0
        ).astype(BF16)

    def fold(block):
        return jnp.concatenate([block[:64, :128], block[64:, 128:]], axis=0)

    def gather(t, cols):
        parts = [kv[t * 128 : t * 128 + 384, cols]]
        for s in range(sides):
            parts.append(kv[512 + 256 * s + 64 * t : 704 + 256 * s + 64 * t, cols])
        return jnp.concatenate(parts, axis=0)

    def pair(half, p):
        lanes = pl.ds(pl.multiple_of(p * 128, 128), 128)
        v_lanes = pl.ds(pl.multiple_of(512 + p * 128, 128), 128)
        inside = p - 2 * half
        k_ext = pl.ds(pl.multiple_of(inside * 128, 128), 128)
        v_ext = pl.ds(pl.multiple_of(256 + inside * 128, 128), 128)
        cuts = [slice(t * 128, t * 128 + 128) for t in range(2)]
        keys = [gather(t, lanes) for t in range(2)]
        values = [gather(t, v_lanes) for t in range(2)]
        query = [diagonal(qs[cut, lanes]) for cut in cuts]
        d_out = [diagonal(da[cut, lanes]) for cut in cuts]
        score = [mm_nt(keys[t], query[t]) + bias[p] for t in range(2)]
        e = [jnp.exp(x - jnp.max(x, axis=0, keepdims=True)) for x in score]
        d_prob = [mm_nt(values[t], d_out[t]) for t in range(2)]
        prob = [x * (1.0 / jnp.sum(x, axis=0, keepdims=True)) for x in e]
        prob_low = [x.astype(BF16) for x in prob]
        attended = [fold(mm(values[t].T, prob_low[t])).astype(BF16) for t in range(2)]
        d_value = [mm(prob_low[t], d_out[t]) for t in range(2)]
        terms = [da[cuts[t], lanes].astype(F32).T * attended[t].astype(F32) for t in range(2)]
        delta = [
            jnp.concatenate(
                [
                    jnp.sum(x[:64], axis=0, keepdims=True),
                    jnp.sum(x[64:], axis=0, keepdims=True),
                ],
                axis=1,
            )
            for x in terms
        ]
        d_score = [prob[t] * (d_prob[t] - delta[t]) for t in range(2)]
        low = [x.astype(BF16) for x in d_score]
        d_query = [fold(mm(keys[t].T, low[t])) * 0.125 for t in range(2)]
        d_key = [mm(low[t], query[t]) for t in range(2)]
        db[p] = d_score[0] + d_score[1]
        for t in range(2):
            att[lanes, cuts[t]] = attended[t]
            dq[cuts[t], lanes] = d_query[t].T.astype(BF16)
        grads = [(d_key[t], d_value[t]) for t in range(2)]
        for kind, cols, wide in ((0, k_ext, lanes), (1, v_ext, v_lanes)):
            g0, g1 = grads[0][kind], grads[1][kind]
            mid = g0[128:384] + g1[:256]
            own[:, wide] = mid
            ext[half, 0:128, cols] = g0[:128].astype(BF16)
            ext[half, 128:384, cols] = mid.astype(BF16)
            ext[half, 384:512, cols] = g1[256:384].astype(BF16)
            for s in range(sides):
                b, e0 = 384 + 192 * s, 512 + 256 * s
                ext[half, e0 : e0 + 64, cols] = g0[b : b + 64].astype(BF16)
                ext[half, e0 + 64 : e0 + 192, cols] = (
                    g0[b + 64 : b + 192] + g1[b : b + 128]
                ).astype(BF16)
                ext[half, e0 + 192 : e0 + 256, cols] = g1[b + 128 : b + 192].astype(BF16)

    def send_back(half):
        src = ext.at[half]
        made = [
            copies.put(src.at[pl.ds(0, 128)], r_o.at[half, 1], (up, ring, dp)),
            copies.put(src.at[pl.ds(384, 128)], r_o.at[half, 0], (down, ring, dp)),
        ]
        for s in range(sides):
            e0 = 512 + 256 * s
            dst, other = r_s.at[half, 0 if sides == 1 else 1 - s], others[s]
            made.append(
                copies.put(src.at[pl.ds(e0, 64)], dst.at[pl.ds(192, 64)], (up, other, dp))
            )
            made.append(
                copies.put(src.at[pl.ds(e0 + 192, 64)], dst.at[pl.ds(0, 64)], (down, other, dp))
            )
            made.append(
                copies.put(src.at[pl.ds(e0 + 64, 128)], dst.at[pl.ds(64, 128)], (az, other, dp))
            )
        return made

    x_first = (False, False, False, True)

    def pair_up(u, grad):
        for c in range(2):
            block = grad[:, c * 256 : c * 256 + 256]
            part[u, c] = block.reshape(rows, rings, share, 256).astype(BF16)
        return copies.put(part.at[u, 1 - core], r1.at[u], (az, ring, mate))

    def spread(u, state):
        state.wait_recv()
        kept = part[u, core].astype(F32) + r1[u].astype(F32)
        if x_first[u]:
            ka[u] = kept.astype(BF16)
            return [
                copies.put(ka.at[u, :, to], rx.at[u, o], (az, to, dp))
                for o, to in enumerate(rng_to)
            ]
        kb[u, 0] = kept[..., :128].astype(BF16)
        kb[u, 1] = kept[..., 128:].astype(BF16)
        return [copies.put(kb.at[u, 1 - y], ry.at[u], (az, ring, over))]

    def cross(u, state):
        for copy in state:
            copy.wait_recv()
        if x_first[u]:
            kept = ka[u, :, ring].astype(F32)
            for o in range(rings - 1):
                kept = kept + rx[u, o].astype(F32)
            two[u, 0] = kept[..., :128].astype(BF16)
            two[u, 1] = kept[..., 128:].astype(BF16)
            return [copies.put(two.at[u, 1 - y], ry2.at[u], (az, ring, over))]
        kb[u, y] = (kb[u, y].astype(F32) + ry[u].astype(F32)).astype(BF16)
        return [
            copies.put(kb.at[u, y, :, to], rx2.at[u, o], (az, to, dp))
            for o, to in enumerate(rng_to)
        ]

    def along(u, state):
        for copy in state:
            copy.wait_recv()
        if x_first[u]:
            kept = two[u, y].astype(F32) + ry2[u].astype(F32)
        else:
            kept = kb[u, y, :, ring].astype(F32)
            for o in range(rings - 1):
                kept = kept + rx2[u, o].astype(F32)
        zin[u] = kept.astype(BF16)
        return [
            copies.put(zin.at[u, to], rz.at[u, o], (to, ring, dp)) for o, to in enumerate(az_to)
        ]

    def collect(u, state):
        for copy in state:
            copy.wait_recv()
        kept = zin[u, az].astype(F32)
        for o in range(rows - 1):
            kept = kept + rz[u, o].astype(F32)
        gath[u, dp] = kept.astype(BF16)
        return [copies.put(gath.at[u, dp], gath.at[u, dp], (az, ring, to)) for to in dp_to]

    def finish(u, state):
        for copy in state:
            copy.wait_recv()
        for d in range(4):
            value = gath[u, d].astype(F32)
            at_y, at_c = (d // 2) * 128, d % 2
            if u == 3:
                go[:, at_c * 256 + at_y : at_c * 256 + at_y + 128] = value
            else:
                start = at_c * 256 if u == 2 else 512 + 512 * at_c + 256 * u
                gq[:, start + at_y : start + at_y + 128] = value

    def looped(half):
        def step(p, carry):
            pair(half, p)
            return carry

        lax.fori_loop(2 * half, 2 * half + 2, step, 0)

    looped(0)
    back = send_back(0)
    u0 = pair_up(0, mm(x_t[...], ext[0]))
    looped(1)
    back += send_back(1)
    u0 = spread(0, u0)
    u1 = pair_up(1, mm(x_t[...], ext[1]))
    u2 = pair_up(2, mm(x_t[:, 128:384], dq[...]))
    u3 = pair_up(3, mm(att[...], cot[...]))
    u1 = spread(1, u1)
    u2 = spread(2, u2)
    u3 = spread(3, u3)

    def unbuild(p, carry):
        for hh in range(2):
            head = 2 * p + hh
            for i in range(17):
                block = jnp.zeros((width, 128), F32)
                for q in range(8):
                    found = [
                        db[p, start : start + size, hh * 128 : hh * 128 + 128]
                        for start, size, _ in pieces(i + q)
                    ]
                    block = jnp.where(group == q, jnp.concatenate(found, axis=0), block)
                tables[pl.ds(pl.multiple_of((i * 8 + head) * width, 8), width), :] = block
        return carry

    lax.fori_loop(0, 4, unbuild, 0)
    total = jnp.zeros((136, 128), F32)
    for c in range(width):
        hot, _ = column(c)
        folded = mm_nt(split(tables[pl.ds(c, 136, width), :], 2), hot)
        total = total + folded[:136] + folded[136:]
    for q in range(4):
        end = min(136, q * 40 + 40)
        bias_mine[0, 0 : end - q * 40, q * 32 : q * 32 + 32] = total[q * 40 : end, 0:32]
    bias_mine[0, 16:40, 96:128] = jnp.zeros((24, 32), F32)
    b = copies.put(bias_mine.at[0], bias_core, (az, ring, mate))
    u0 = cross(0, u0)
    u1 = cross(1, u1)
    b.wait_recv()
    bias_mine[1] = bias_mine[0] + bias_core[...]
    b = copies.put(bias_mine.at[1], bias_y, (az, ring, over))
    u2 = cross(2, u2)
    u3 = cross(3, u3)
    b.wait_recv()
    bias_x[ring] = bias_mine[1] + bias_y[...]
    b = [copies.put(bias_x.at[ring], bias_x.at[ring], (az, to, dp)) for to in rng_to]
    u0 = along(0, u0)
    u1 = along(1, u1)
    for copy in b:
        copy.wait_recv()
    bias_z[az] = functools.reduce(jnp.add, [bias_x[r] for r in range(rings)])
    b = [copies.put(bias_z.at[az], bias_z.at[az], (to, ring, dp)) for to in az_to]
    u2 = along(2, u2)
    u3 = along(3, u3)
    u0 = collect(0, u0)
    u1 = collect(1, u1)

    for copy in back:
        copy.wait_recv()
    grads = []
    zero = jnp.zeros((16, 8, 512), F32)
    for half in range(2):
        grad = jnp.concatenate([r_o[half, 0], r_o[half, 1]], axis=0).astype(F32)
        mids = []
        for s in range(sides):
            got = r_s[half, s].astype(F32)
            mid = got[64:192] + jnp.concatenate([got[0:64], got[192:256]], axis=0)
            mids.append(mid.reshape(16, 8, 512))
        if sides == 1:
            low = jnp.where(ring == 0, zero, mids[0])
            high = jnp.where(ring == 0, mids[0], zero)
        else:
            low, high = mids
        grads.append(grad + jnp.concatenate([low, high], axis=1).reshape(256, 512))
    d_key = own[:, :512] + jnp.concatenate([grads[0][:, :256], grads[1][:, :256]], axis=1)
    d_value = own[:, 512:] + jnp.concatenate([grads[0][:, 256:], grads[1][:, 256:]], axis=1)
    gtok[...] = (
        mm_nt(dq[...], wqkv[:, :512])
        + mm_nt(d_key.astype(BF16), wqkv[:, 512:1024])
        + mm_nt(d_value.astype(BF16), wqkv[:, 1024:])
    ).astype(BF16)
    u2 = collect(2, u2)
    u3 = collect(3, u3)
    for copy in b:
        copy.wait_recv()
    summed = functools.reduce(jnp.add, [bias_z[a] for a in range(rows)])
    for q in range(4):
        end = min(136, q * 40 + 40)
        gb_ref[q * 40 : end, 0:32] = summed[0 : end - q * 40, q * 32 : q * 32 + 32]
    finish(0, u0)
    finish(1, u1)
    finish(2, u2)
    finish(3, u3)
    copies.drain()


def leave_kernel(*refs):
    source, target, held, sem = refs[:4], refs[4:8], refs[8:12], refs[12]
    loads = [pltpu.make_async_copy(source[i], held[i], sem.at[i]) for i in range(4)]
    for load in loads:
        load.start()
    stores = []
    for i in range(3):
        loads[i].wait()
        stores.append(pltpu.make_async_copy(held[i], target[i], sem.at[4 + i]))
        stores[-1].start()
    loads[3].wait()
    target[3][...] = held[3][:, 0:17].reshape(17, 8, 17)
    for store in stores:
        store.wait()


def shards(rows, rings, tokens, qkv_weight, out_weight, relative_bias, cotangent):
    sides = 1 if rings == 2 else 2
    share = 512 // (rows * rings)
    tok, cot = tokens.reshape(256, 512), cotangent.reshape(256, 512)
    shape = jax.ShapeDtypeStruct
    sems = pltpu.SemaphoreType.DMA
    count = 2 + 3 * sides + 2 * (2 + 3 * sides)
    count += 4 * (1 + rings + rows + 2) + 2 + (rings - 1) + (rows - 1)
    keys, cells = 384 + 192 * sides, 512 + 256 * sides

    def low(*dims):
        return pltpu.VMEM(dims, BF16)

    def full(*dims):
        return pltpu.VMEM(dims, F32)

    hbm = pl.BlockSpec(memory_space=pltpu.HBM)
    vmem = pl.BlockSpec(memory_space=pltpu.VMEM)
    made = pl.pallas_call(
        functools.partial(fused_kernel, rows, rings, sides, share),
        out_shape=(
            shape((256, 512), BF16),
            shape((share, 1536), F32),
            shape((share, 512), F32),
            shape((136, 128), F32),
        ),
        in_specs=[hbm] * 5,
        out_specs=(vmem, vmem, vmem, vmem),
        scratch_shapes=[
            low(512, 512),
            low(sides, 256, 512),
            low(sides, 128, 512),
            low(512, 1536),
            low(512, 512),
            low(256, 512),
            full(17, 8, 17),
            low(512, cells),
            low(cells, 1024),
            low(256, 512),
            low(256, 512),
            full(136, 128),
            full(136 * (16 + 8 * sides), 128),
            full(4, keys, 256),
            full(4, keys, 256),
            low(256, 512),
            low(512, 256),
            full(256, 1024),
            low(2, cells, 512),
            low(2, 2, 128, 512),
            low(2, sides, 256, 512),
            low(4, 2, rows, rings, share, 256),
            low(4, rows, rings, share, 256),
            low(4, rows, rings, share, 256),
            low(4, 2, rows, rings, share, 128),
            low(4, rings - 1, rows, share, 256),
            low(4, rows, rings, share, 128),
            low(4, 2, rows, share, 128),
            low(4, rows, share, 128),
            low(4, rings - 1, rows, share, 128),
            low(4, rows, share, 128),
            low(4, rows - 1, share, 128),
            low(4, 4, share, 128),
            full(2, 40, 128),
            full(40, 128),
            full(40, 128),
            full(rings, 40, 128),
            full(rows, 40, 128),
            sems((count,)),
            sems((count,)),
            sems((5,)),
        ],
        compiler_params=pltpu.CompilerParams(
            collective_id=0, has_side_effects=True, vmem_limit_bytes=62 * 1024 * 1024
        ),
        name="fused",
    )(tok, qkv_weight, out_weight, relative_bias.transpose(1, 0, 2), cot)
    gtok, gq, go, gb = pl.pallas_call(
        leave_kernel,
        out_shape=tuple(shape(x.shape, x.dtype) for x in made[:3]) + (shape((17, 8, 17), F32),),
        in_specs=[hbm] * 4,
        out_specs=(hbm, hbm, hbm, vmem),
        scratch_shapes=[pltpu.VMEM(x.shape, x.dtype) for x in made] + [sems((8,))],
        compiler_params=pltpu.CompilerParams(vmem_limit_bytes=62 * 1024 * 1024),
        name="leave",
    )(*made)
    return gtok.reshape(tokens.shape), gq, go, gb.transpose(1, 0, 2)


def solution(mesh):
    placed = (P("dp", "az", "rng", None), P(), P(), P(), P("dp", "az", "rng", None))
    return jax.shard_map(
        functools.partial(shards, mesh.shape["az"], mesh.shape["rng"]),
        mesh=mesh,
        in_specs=placed,
        out_specs=(P("dp", "az", "rng", None), P(("az", "rng"), None), P(("az", "rng"), None), P()),
        check_vma=False,
    )
```
